128 devices in a mesh: member: 4 (over y_lo, core), space: 32 (over y_hi, z, x).
Axes of the slice: x: 4, y: 4 (y_hi: 2, y_lo: 2; y = y_hi * 2 + y_lo), z: 4, core: 2. Of those that a mesh axis runs over, the one named last changes fastest.
Arguments:
- latent: bfloat16 [4, 65536, 1024], P('member', 'space'), may hold values from -6 to 6
- target: float32 [100, 65536], P(None, 'space'), may hold values from -6 to 6
- area_weight: float32 [65536], P('space'), may hold values from 0.2 to 3.1, as said below
- var_weight: float32 [100], replicated, may hold values from 0.3 to 3
- w_hidden: bfloat16 [1024, 1024], replicated, may hold values from -0.1875 to 0.1875
- b_hidden: float32 [1024], replicated, may hold values from -3 to 3
- w_output: bfloat16 [100, 1024], replicated, may hold values from -0.1875 to 0.1875
- b_output: float32 [100], replicated, may hold values from -3 to 3
Outputs:
- loss: float32 [], replicated
- grad_w_hidden: float32 [1024, 1024], replicated
- grad_b_hidden: float32 [1024], replicated
- grad_w_output: float32 [100, 1024], replicated
- grad_b_output: float32 [100], replicated
- latent_grad: bfloat16 [4, 65536, 1024], P('member', 'space')
The draws below stay inside these ranges and needn't reach their ends.
Inputs may be any that keep to these rules, and one draw needn't show every extreme that they name: `area_weight`: positive.
All inputs are finite; a program needn't handle non-finite values.
Results may differ from the reference program's by a relative error of at most 0.003.
The reference program's roundings to bfloat16 on the way (of `hid`, `cot` and `dpre`) count: a program that leaves them out, or rounds other values in their place, can miss the bound.
Values sent between devices are 32-bit elements; how exact they have to be, the bound alone decides.
No kernel may reach another device: no remote copies, remote signals or barrier semaphores. Data moves between devices by JAX's collectives and lax.ppermute only.
A program may use at most 128 MiB of HBM per device.

```python
import math
import jax
import jax.numpy as jnp
from jax import lax

D = 1024
V = 100
MEMBERS = 4
POINTS = 65536


def draw_area_weight(key, part):
    key = jax.random.fold_in(key, 11)
    place = jnp.arange(POINTS, dtype=jnp.float32) / jnp.float32(max(POINTS - 1, 1))
    trend = 0.5 * jnp.exp(jnp.log(3.0) * place)
    noise = jax.random.uniform(key, (POINTS,), jnp.float32, -0.35, 0.35)
    return (trend * jnp.exp(noise)).astype(jnp.float32)


def block_levels(key, extent, split, low, high):
    def one(axis_at, parts):
        draws = jax.random.uniform(jax.random.fold_in(jax.random.fold_in(key, 6), axis_at), (parts,), jnp.float32, low / len(split), high / len(split))
        return jnp.repeat(jnp.exp(draws), extent[axis_at] // parts).reshape((-1,) + (1,) * (len(extent) - axis_at - 1))

    level = one(*split[0])
    for cut in split[1:]:
        level = level * one(*cut)
    return level


def centred(rng, shape, deviation, limit, pieces=(), held_as=jnp.bfloat16):
    gain = block_levels(rng, shape, pieces, -0.22, 0.18) if pieces else 1.0
    result = jax.random.normal(rng, shape, jnp.float32) * deviation * gain
    return jnp.minimum(jnp.maximum(result, -limit), limit).astype(held_as)


def setup_inputs(seed: int = 0) -> dict:
    key_of = jax.random.split(jax.random.key(seed), 9)
    return {
        "latent": centred(key_of[0], (MEMBERS, POINTS, D), 1.0, 6.0, ((0, 4), (1, 32))),
        "target": centred(key_of[1], (V, POINTS), 1.0, 6.0, ((1, 32),), jnp.float32),
        "area_weight": draw_area_weight(jax.random.fold_in(key_of[8], 71), 0),
        "var_weight": jnp.clip(jnp.exp(jax.random.uniform(key_of[3], (V,), jnp.float32, math.log(0.3), math.log(3.0))), 0.3, 3.0),
        "w_hidden": centred(key_of[4], (D, D), D ** -0.5, 0.1875),
        "b_hidden": centred(key_of[5], (D,), 0.5, 3.0, (), jnp.float32),
        "w_output": centred(key_of[6], (V, D), D ** -0.5, 0.1875),
        "b_output": centred(key_of[7], (V,), 0.5, 3.0, (), jnp.float32),
    }


DELTA = 0.05

def smooth(diff):
    return jnp.sqrt(diff * diff + DELTA * DELTA) - DELTA

def slope(diff):
    return diff / jnp.sqrt(diff * diff + DELTA * DELTA)

def reference(latent, target, area_weight, var_weight, w_hidden, b_hidden, w_output, b_output):
    eps = 0.05 / MEMBERS
    pair_coef = (1.0 - eps) / (MEMBERS * (MEMBERS - 1))
    scale_root = jnp.sqrt(jnp.float32(MEMBERS * POINTS))
    weights = var_weight[:, None] * area_weight[None, :]
    pres = []
    hids = []
    preds = []
    for member in range(MEMBERS):
        pre = jnp.dot(latent[member], w_hidden, preferred_element_type=jnp.float32) + b_hidden
        hid = jax.nn.silu(pre).astype(jnp.bfloat16)
        pred = jnp.dot(w_output, hid.T, preferred_element_type=jnp.float32) + b_output[:, None]
        pres.append(pre)
        hids.append(hid)
        preds.append(pred)
    loss = jnp.float32(0.0)
    grad_w_hidden = jnp.zeros((D, D), jnp.float32)
    grad_b_hidden = jnp.zeros((D,), jnp.float32)
    grad_w_output = jnp.zeros((V, D), jnp.float32)
    grad_b_output = jnp.zeros((V,), jnp.float32)
    latent_grads = []
    for member in range(MEMBERS):
        own = preds[member]
        pair_mag = jnp.zeros_like(own)
        pair_slope = jnp.zeros_like(own)
        for other in range(MEMBERS):
            diff = own - preds[other]
            pair_mag = pair_mag + smooth(diff)
            pair_slope = pair_slope + slope(diff)
        term = smooth(own - target) / MEMBERS - 0.5 * pair_coef * pair_mag
        loss = loss + jnp.sum(weights * term) / (POINTS * V)
        cot = (weights * (slope(own - target) / MEMBERS - pair_coef * pair_slope)).astype(jnp.bfloat16)
        grad_b_output = grad_b_output + lax.optimization_barrier(jnp.sum(cot.astype(jnp.float32), axis=1))
        grad_w_output = grad_w_output + jnp.dot(cot, hids[member], preferred_element_type=jnp.float32)
        back = jnp.dot(cot.T, w_output, preferred_element_type=jnp.float32)
        sig = jax.nn.sigmoid(pres[member])
        dpre = (back * sig * (1.0 + pres[member] * (1.0 - sig))).astype(jnp.bfloat16)
        grad_b_hidden = grad_b_hidden + lax.optimization_barrier(jnp.sum(dpre.astype(jnp.float32), axis=0))
        grad_w_hidden = grad_w_hidden + jnp.dot(latent[member].T, dpre, preferred_element_type=jnp.float32)
        latent_grads.append(jnp.dot(dpre, w_hidden.T, preferred_element_type=jnp.float32).astype(jnp.bfloat16))
    latent_grad = jnp.stack(latent_grads, axis=0)
    return (loss, grad_w_hidden / scale_root, grad_b_hidden / scale_root, grad_w_output / scale_root, grad_b_output / scale_root, latent_grad)
```

```python
import math

import jax
import jax.numpy as jnp
from jax import lax
from jax.sharding import Mesh, PartitionSpec as P

DELTA = 0.05
ALL = ("ylo", "core", "yhi", "z", "x")


def flat(core, x, y, z):
    return ((y % 2) * 2 + core) * 32 + (y // 2) * 16 + z * 4 + x


def moved(where):
    pairs = []
    for core in range(2):
        for x in range(4):
            for y in range(4):
                for z in range(4):
                    pairs.append((flat(core, x, y, z), flat(*where(core, x, y, z))))
    return pairs


SWAP = moved(lambda c, x, y, z: (1 - c, x, y, z))
NEAR = moved(lambda c, x, y, z: (c, x, y ^ 1, z))


def first(k):
    return moved(lambda c, x, y, z: (c, x, y, (z + k) % 4) if c == 0 else (c, (x + k) % 4, y, z))


def second(k):
    return moved(lambda c, x, y, z: (c, x, y, (z + k) % 4) if c == 1 else (c, (x + k) % 4, y, z))


def along_y(k):
    return moved(lambda c, x, y, z: (c, x, (y + k) % 4, z))


def send(array, pairs):
    return lax.ppermute(array, ALL, pairs)


def grad_sum(own, sibling):
    core, x, z = lax.axis_index("core"), lax.axis_index("x"), lax.axis_index("z")
    place = jnp.where(core == 0, x, z)
    got = send(sibling, SWAP)
    held = [own[k] + got[k] for k in range(4)]
    block = held[0]
    for k in (1, 3, 2):
        block = block + send(held[k], first(k))
    rows = block.shape[0] // 4
    quarters = block.reshape((4, rows) + block.shape[1:])
    pick = lambda k: lax.dynamic_index_in_dim(quarters, (place + k) % 4, 0, keepdims=False)
    quarter = pick(0)
    for k in (1, 3, 2):
        quarter = quarter + send(pick(k), second(k))
    quarter = quarter + send(quarter, along_y(1)) + send(quarter, along_y(3)) + send(quarter, along_y(2))
    came = [quarter] + [send(quarter, second(k)) for k in (1, 2, 3)]
    twice = jnp.concatenate([came[3], came[2], came[1], came[0], came[3], came[2], came[1]], 0)
    block = lax.dynamic_slice_in_dim(twice, ((3 - place) % 4) * rows, 4 * rows, 0)
    mine = [block] + [send(block, first(k)) for k in (1, 2, 3)]
    return mine, [send(m, SWAP) for m in mine]


def smooth(diff):
    return jnp.sqrt(diff * diff + DELTA * DELTA) - DELTA


def slope(diff):
    return diff / jnp.sqrt(diff * diff + DELTA * DELTA)


def shards(latent, target, area_weight, var_weight, w_hidden, b_hidden, w_output, b_output):
    members = 4
    n_vars, points = target.shape
    points_all = points * 32
    depth, width = w_hidden.shape
    eps = 0.05 / members
    pair_coef = (1.0 - eps) / (members * (members - 1))
    scale = 1.0 / math.sqrt(members * points_all)
    core, x, z = lax.axis_index("core"), lax.axis_index("x"), lax.axis_index("z")
    place_own = jnp.where(core == 0, z, x)
    place_sib = jnp.where(core == 0, x, z)
    own_latent = latent[0]
    pre = jnp.dot(own_latent, w_hidden, preferred_element_type=jnp.float32) + b_hidden
    sig = jax.nn.sigmoid(pre)
    hid = (pre * sig).astype(jnp.bfloat16)
    own = (
        lax.dot_general(w_output, hid, (((1,), (1,)), ((), ())), preferred_element_type=jnp.float32)
        + b_output[:, None]
    )
    near = send(own, NEAR)
    others = (send(own, SWAP), near, send(near, SWAP))
    pair_mag = sum(smooth(own - other) for other in others)
    pair_slope = sum(slope(own - other) for other in others)
    weights = var_weight[:, None] * area_weight[None, :]
    term = smooth(own - target) / members - 0.5 * pair_coef * pair_mag
    loss_part = jnp.sum(weights * term) / (points_all * n_vars)
    cot = (weights * (slope(own - target) / members - pair_coef * pair_slope)).astype(jnp.bfloat16)
    part_b_output = jnp.sum(cot.astype(jnp.float32), axis=1) * scale
    part_w_output = jnp.dot(cot, hid, preferred_element_type=jnp.float32) * scale
    back = lax.dot_general(
        cot, w_output, (((0,), (0,)), ((), ())), preferred_element_type=jnp.float32
    )
    dpre = (back * sig * (1.0 + pre * (1.0 - sig))).astype(jnp.bfloat16)
    part_b_hidden = jnp.sum(dpre.astype(jnp.float32), axis=0) * scale
    part_w_hidden = (
        lax.dot_general(
            own_latent, dpre, (((0,), (0,)), ((), ())), preferred_element_type=jnp.float32
        )
        * scale
    )
    misc = jnp.concatenate([part_b_output, loss_part[None], jnp.zeros((width - n_vars - 1,), jnp.float32)])
    rest = jnp.concatenate(
        [part_w_output, part_b_hidden[None], misc[None], jnp.zeros((128 - n_vars - 2, width), jnp.float32)], 0
    )
    blocks = jnp.concatenate([part_w_hidden.reshape(4, depth // 4, width), rest.reshape(4, 32, width)], 1)
    half = width // 2

    def ordered(which, place):
        mine = lax.dynamic_slice_in_dim(blocks, which * half, half, 2)
        twice = jnp.concatenate([mine, mine[:3]], 0)
        return lax.dynamic_slice_in_dim(twice, place, 4, 0)

    out_own, out_sib = grad_sum(ordered(core, place_own), ordered(1 - core, place_sib))
    latent_grad = lax.dot_general(
        dpre, w_hidden, (((1,), (1,)), ((), ())), preferred_element_type=jnp.float32
    ).astype(jnp.bfloat16)

    def in_place(outs, place):
        return jnp.take(jnp.stack(outs), (place - jnp.arange(4)) % 4, axis=0)

    o, s = in_place(out_own, place_own), in_place(out_sib, place_sib)
    whole = jnp.concatenate([jnp.where(core == 0, o, s), jnp.where(core == 0, s, o)], 2)
    grad_w_hidden = whole[:, : depth // 4].reshape(depth, width)
    rest = whole[:, depth // 4 :].reshape(128, width)
    return (
        rest[n_vars + 1, n_vars],
        grad_w_hidden,
        rest[n_vars],
        rest[:n_vars],
        rest[n_vars + 1, :n_vars],
        latent_grad[None],
    )


def solution(mesh):
    fine = Mesh(mesh.devices.reshape(2, 2, 2, 4, 4), ALL)
    member, space = ("ylo", "core"), ("yhi", "z", "x")
    return jax.shard_map(
        shards,
        mesh=fine,
        in_specs=(P(member, space, None), P(None, space), P(space), P(), P(), P(), P(), P()),
        out_specs=(P(), P(), P(), P(), P(), P(member, space, None)),
        check_vma=False,
    )
```

```python
import functools
import math

import jax
import jax.numpy as jnp
from jax import lax
from jax.experimental import pallas as pl
from jax.experimental.pallas import tpu as pltpu
from jax.sharding import Mesh, PartitionSpec as P

DELTA = 0.05
ALL = ("ylo", "core", "yhi", "z", "x")
MIB = 1 << 20
F32, BF16 = jnp.float32, jnp.bfloat16


def flat(core, x, y, z):
    return ((y % 2) * 2 + core) * 32 + (y // 2) * 16 + z * 4 + x


def moved(where):
    pairs = []
    for core in range(2):
        for x in range(4):
            for y in range(4):
                for z in range(4):
                    pairs.append((flat(core, x, y, z), flat(*where(core, x, y, z))))
    return pairs


SWAP = moved(lambda c, x, y, z: (1 - c, x, y, z))
NEAR = moved(lambda c, x, y, z: (c, x, y ^ 1, z))


def first(k):
    return moved(lambda c, x, y, z: (c, x, y, (z + k) % 4) if c == 0 else (c, (x + k) % 4, y, z))


def second(k):
    return moved(lambda c, x, y, z: (c, x, y, (z + k) % 4) if c == 1 else (c, (x + k) % 4, y, z))


def along_y(k):
    return moved(lambda c, x, y, z: (c, x, (y + k) % 4, z))


def send(array, pairs):
    return lax.ppermute(array, ALL, pairs)


def grad_sum(own, sibling):
    core, x, z = lax.axis_index("core"), lax.axis_index("x"), lax.axis_index("z")
    place = jnp.where(core == 0, x, z)
    got = send(sibling, SWAP)
    held = [own[k] + got[k] for k in range(4)]
    block = held[0]
    for k in (1, 3, 2):
        block = block + send(held[k], first(k))
    rows = block.shape[0] // 4
    quarters = block.reshape((4, rows) + block.shape[1:])
    pick = lambda k: lax.dynamic_index_in_dim(quarters, (place + k) % 4, 0, keepdims=False)
    quarter = pick(0)
    for k in (1, 3, 2):
        quarter = quarter + send(pick(k), second(k))
    quarter = quarter + send(quarter, along_y(1)) + send(quarter, along_y(3)) + send(quarter, along_y(2))
    came = [quarter] + [send(quarter, second(k)) for k in (1, 2, 3)]
    twice = jnp.concatenate([came[3], came[2], came[1], came[0], came[3], came[2], came[1]], 0)
    block = lax.dynamic_slice_in_dim(twice, ((3 - place) % 4) * rows, 4 * rows, 0)
    mine = [block] + [send(block, first(k)) for k in (1, 2, 3)]
    return mine, [send(m, SWAP) for m in mine]


def params(mib):
    return pltpu.CompilerParams(vmem_limit_bytes=mib * MIB)


def cost(flops, moved_bytes, trans=0):
    return pl.CostEstimate(flops=flops, bytes_accessed=moved_bytes, transcendentals=trans)


def forward_kernel(lat, w, b_hid, w_out, b_out, *refs):
    pred, hid, slope_out = refs[-3:]
    pre = jnp.dot(lat[...], w[...], preferred_element_type=F32) + b_hid[...]
    sig = jax.nn.sigmoid(pre)
    h = (pre * sig).astype(BF16)
    hid[...] = h
    slope_out[...] = sig * (1.0 + pre * (1.0 - sig))
    turned = lax.dot_general(h, w_out[...], (((1,), (1,)), ((), ())), preferred_element_type=F32)
    pred[...] = jnp.transpose(turned + b_out[...])


def forward(part, parts, tile, latent, w_hidden, b_hidden, w_output, b_output, held):
    points, depth = latent.shape
    width, n_vars = w_hidden.shape[1], w_output.shape[0]
    n = points // parts
    steps = n // tile
    whole = lambda shape: pl.BlockSpec(shape, lambda g: (0,) * len(shape))
    rows = lambda cols: pl.BlockSpec((tile, cols), lambda g: (part * steps + g, 0))
    return pl.pallas_call(
        forward_kernel,
        grid=(steps,),
        in_specs=[rows(depth), whole(w_hidden.shape), whole((1, width)), whole(w_output.shape), whole((1, n_vars))]
        + [pl.BlockSpec(memory_space=pl.ANY)] * len(held),
        out_specs=[pl.BlockSpec((n_vars, tile), lambda g: (0, g)), rows(width), rows(width)],
        out_shape=[
            jax.ShapeDtypeStruct((n_vars, n), F32),
            jax.ShapeDtypeStruct((points, width), BF16),
            jax.ShapeDtypeStruct((points, width), F32),
        ],
        input_output_aliases={5: 1, 6: 2} if held else {},
        compiler_params=params(40),
        cost_estimate=cost(2 * n * width * (depth + n_vars), n * (2 * depth + 6 * width) + 2 * depth * width, 2 * n * width),
    )(latent, w_hidden, b_hidden.reshape(1, width), w_output, b_output.reshape(1, n_vars), *held)


def turn_kernel(a, _, out):
    out[...] = jnp.transpose(a[...])


def turn(a, after):
    rows, cols = a.shape
    br, bc = 1024, 256
    return pl.pallas_call(
        turn_kernel,
        grid=(cols // bc, rows // br),
        in_specs=[pl.BlockSpec((br, bc), lambda i, j: (j, i)), pl.BlockSpec(memory_space=pl.ANY)],
        out_specs=pl.BlockSpec((bc, br), lambda i, j: (i, j)),
        out_shape=jax.ShapeDtypeStruct((cols, rows), a.dtype),
        compiler_params=params(40),
        cost_estimate=cost(0, 4 * rows * cols),
    )(a, after)


def cot_kernel(members, loss_scale, pair_coef, own, o1, o2, o3, target, area, var, *refs):
    cot, turned, misc, pad = refs[-4:]
    n_vars = own.shape[0]
    weights = var[...] * area[...]
    mine = own[...]

    def both(diff):
        u = diff * diff + DELTA * DELTA
        r = lax.rsqrt(u)
        return u * r - DELTA, diff * r

    mag, slo = both(mine - target[...])
    pair_mag, pair_slo = jnp.zeros_like(mine), jnp.zeros_like(mine)
    for other in (o1, o2, o3):
        m, s = both(mine - other[...])
        pair_mag, pair_slo = pair_mag + m, pair_slo + s
    term = weights * (mag * (1.0 / members) - (0.5 * pair_coef) * pair_mag)
    rounded = (weights * (slo * (1.0 / members) - pair_coef * pair_slo)).astype(BF16)
    cot[...] = rounded
    pad[...] = jnp.zeros_like(pad)
    pad[0:n_vars, :] = rounded.astype(F32)
    t = jnp.transpose(pad[...])
    turned[...] = t.astype(BF16)
    lane = lax.broadcasted_iota(jnp.int32, (1, 128), 1)
    sums = jnp.sum(t, axis=0, keepdims=True) + jnp.where(lane == n_vars, jnp.sum(term) * loss_scale, 0.0)

    @pl.when(pl.program_id(0) == 0)
    def _():
        misc[...] = jnp.zeros_like(misc)

    misc[...] += sums


def cotangent(part, parts, tile, own, others, target, area, var, held, members, loss_scale, pair_coef):
    n_vars, points = target.shape
    n = points // parts
    steps = n // tile
    local = pl.BlockSpec((n_vars, tile), lambda g: (0, g))
    placed = pl.BlockSpec((n_vars, tile), lambda g: (0, part * steps + g))
    return pl.pallas_call(
        functools.partial(cot_kernel, members, loss_scale, pair_coef),
        grid=(steps,),
        in_specs=[local] * 4
        + [placed, pl.BlockSpec((1, tile), lambda g: (0, part * steps + g)), pl.BlockSpec((n_vars, 1), lambda g: (0, 0))]
        + [pl.BlockSpec(memory_space=pl.ANY)] * len(held),
        out_specs=[
            placed,
            pl.BlockSpec((tile, 128), lambda g: (part * steps + g, 0)),
            pl.BlockSpec((1, 128), lambda g: (0, 0)),
        ],
        out_shape=[
            jax.ShapeDtypeStruct((n_vars, points), BF16),
            jax.ShapeDtypeStruct((points, 128), BF16),
            jax.ShapeDtypeStruct((1, 128), F32),
        ],
        scratch_shapes=[pltpu.VMEM((128, tile), F32)],
        input_output_aliases={7: 0, 8: 1} if held else {},
        compiler_params=params(40),
        cost_estimate=cost(60 * n * n_vars, n * n_vars * 24, 4 * n * n_vars),
    )(own, *others, target, area, var, *held)


def backward_kernel(scale, chunks, where, cot, turned, sp, hid, w_out, lat, misc0, misc1, dpre, out, dall, rest):
    g = pl.program_id(0)
    n_vars, tile = cot.shape
    row = lax.broadcasted_iota(jnp.int32, rest.shape, 0)

    @pl.when(g == 0)
    def _():
        m = jnp.concatenate([misc0[...] + misc1[...]] * (rest.shape[1] // 128), axis=1)
        kept = jnp.where(lax.broadcasted_iota(jnp.int32, m.shape, 1) == n_vars, m, m * scale)
        rest[...] = jnp.where(row == n_vars + 1, kept, 0.0)

    @pl.when(g < chunks)
    def _():
        back = jnp.dot(turned[...], w_out[...], preferred_element_type=F32)
        d = (back * sp[...]).astype(BF16)
        dall[pl.ds(pl.multiple_of(g * tile, tile), tile), :] = d
        dpre[...] = d
        rest[0:n_vars, :] += jnp.dot(cot[...], hid[...], preferred_element_type=F32) * scale
        rest[n_vars : n_vars + 1, :] += jnp.sum(d.astype(F32), axis=0, keepdims=True) * scale

    @pl.when(g >= chunks)
    def _():
        block = lax.rem(where[1] + g - chunks, 4)
        rows = lat.shape[0]
        out[0, 0:rows, :] = jnp.dot(lat[...], dall[...], preferred_element_type=F32) * scale
        out[0, rows : rows + 32, :] = rest[pl.ds(pl.multiple_of(block * 32, 32), 32), :]


def backward(which, place, cot, turned, sp, hid, w_out, lat_t, misc, scale, tile=512):
    n_vars, points = cot.shape
    depth, width = lat_t.shape[0], hid.shape[1]
    half, rows, chunks = width // 2, depth // 4, points // tile
    at = lambda g: jnp.minimum(g, chunks - 1)
    step = lambda g: jnp.maximum(g - chunks, 0)
    return pl.pallas_call(
        functools.partial(backward_kernel, scale, chunks),
        grid_spec=pltpu.PrefetchScalarGridSpec(
            num_scalar_prefetch=1,
            grid=(chunks + 4,),
            in_specs=[
                pl.BlockSpec((n_vars, tile), lambda g, s: (0, at(g))),
                pl.BlockSpec((tile, 128), lambda g, s: (at(g), 0)),
                pl.BlockSpec((tile, half), lambda g, s: (at(g), s[0])),
                pl.BlockSpec((tile, half), lambda g, s: (at(g), s[0])),
                pl.BlockSpec((128, half), lambda g, s: (0, s[0])),
                pl.BlockSpec((rows, points), lambda g, s: (lax.rem(s[1] + step(g), 4), 0)),
                pl.BlockSpec((1, 128), lambda g, s: (0, 0)),
                pl.BlockSpec((1, 128), lambda g, s: (0, 0)),
            ],
            out_specs=[
                pl.BlockSpec((tile, half), lambda g, s: (at(g), 0)),
                pl.BlockSpec((1, rows + 32, half), lambda g, s: (step(g), 0, 0)),
            ],
            scratch_shapes=[pltpu.VMEM((points, half), BF16), pltpu.VMEM((128, half), F32)],
        ),
        out_shape=[
            jax.ShapeDtypeStruct((points, half), BF16),
            jax.ShapeDtypeStruct((4, rows + 32, half), F32),
        ],
        compiler_params=params(40),
        cost_estimate=cost(2 * points * half * (depth + 2 * n_vars), points * (8 * half + 2 * depth), 0),
    )(jnp.stack([which, place]).astype(jnp.int32), cot, turned, sp, hid, w_out, lat_t, *misc)


def latent_kernel(where, d0, d1, w0, w1, out):
    dims = (((1,), (1,)), ((), ()))
    out[0] = (
        lax.dot_general(d0[...], w0[...], dims, preferred_element_type=F32)
        + lax.dot_general(d1[...], w1[...], dims, preferred_element_type=F32)
    ).astype(BF16)


def latent_gradient(core, dpre_own, dpre_sib, w_hidden, tile=512):
    points, half = dpre_own.shape
    depth = w_hidden.shape[0]
    rows = pl.BlockSpec((tile, half), lambda g, s: (g, 0))
    return pl.pallas_call(
        latent_kernel,
        grid_spec=pltpu.PrefetchScalarGridSpec(
            num_scalar_prefetch=1,
            grid=(points // tile,),
            in_specs=[
                rows,
                rows,
                pl.BlockSpec((depth, half), lambda g, s: (0, s[0])),
                pl.BlockSpec((depth, half), lambda g, s: (0, 1 - s[0])),
            ],
            out_specs=pl.BlockSpec((1, tile, depth), lambda g, s: (0, g, 0)),
        ),
        out_shape=jax.ShapeDtypeStruct((1, points, depth), BF16),
        compiler_params=params(40),
        cost_estimate=cost(4 * points * half * depth, points * (4 * half + 2 * depth) + 4 * depth * half, 0),
    )(core[None].astype(jnp.int32), dpre_own, dpre_sib, w_hidden, w_hidden)


def join_kernel(n_vars, where, *refs):
    ins, (grad_w, grad_o, grad_b, misc, rest) = refs[:8], refs[8:]
    rows, half = ins[0].shape[0] - 32, ins[0].shape[1]
    for which in range(2):
        col = where[0] if which == 0 else 1 - where[0]
        cols = pl.ds(pl.multiple_of(col * half, half), half)
        for k in range(4):
            block = lax.rem(where[1 + which] - k + 4, 4)
            grad_w[pl.ds(pl.multiple_of(block * rows, rows), rows), cols] = ins[4 * which + k][0:rows, :]
            rest[pl.ds(pl.multiple_of(block * 32, 32), 32), cols] = ins[4 * which + k][rows : rows + 32, :]
    grad_o[...] = rest[0:n_vars, :]
    grad_b[...] = rest[n_vars : n_vars + 1, :]
    misc[...] = rest[n_vars + 1 : n_vars + 2, 0:128]


def join(core, place_own, place_sib, own, sib, n_vars):
    rows, half = own[0].shape
    depth, width = 4 * (rows - 32), 2 * half
    vmem = pl.BlockSpec(memory_space=pltpu.VMEM)
    return pl.pallas_call(
        functools.partial(join_kernel, n_vars),
        in_specs=[pl.BlockSpec(memory_space=pltpu.SMEM)] + [vmem] * 8,
        out_specs=[vmem] * 4,
        out_shape=[
            jax.ShapeDtypeStruct((depth, width), F32),
            jax.ShapeDtypeStruct((n_vars, width), F32),
            jax.ShapeDtypeStruct((1, width), F32),
            jax.ShapeDtypeStruct((1, 128), F32),
        ],
        scratch_shapes=[pltpu.VMEM((128, width), F32)],
        compiler_params=params(40),
        cost_estimate=cost(0, 8 * depth * width, 0),
    )(jnp.stack([core, place_own, place_sib]).astype(jnp.int32), *own, *sib)


def shards(latent, target, area_weight, var_weight, w_hidden, b_hidden, w_output, b_output):
    members, parts, tile = 4, 2, 512
    n_vars, points = target.shape
    points_all = points * 32
    eps = 0.05 / members
    pair_coef = (1.0 - eps) / (members * (members - 1))
    scale = 1.0 / math.sqrt(members * points_all)
    core, x, z = lax.axis_index("core"), lax.axis_index("x"), lax.axis_index("z")
    place_own = jnp.where(core == 0, z, x)
    place_sib = jnp.where(core == 0, x, z)
    own_latent = latent[0]
    preds, held = [], ()
    for part in range(parts):
        pred, *held = forward(part, parts, tile, own_latent, w_hidden, b_hidden, w_output, b_output, held)
        preds.append(pred)
    hid, sp = held
    near = [send(p, NEAR) for p in preds]
    sibling = [send(p, SWAP) for p in preds]
    near_sibling = [send(p, SWAP) for p in near]
    lat_t = turn(own_latent, preds[-1])
    area, var = area_weight.reshape(1, points), var_weight.reshape(n_vars, 1)
    w_padded = jnp.pad(w_output, ((0, 128 - n_vars), (0, 0)))
    held, misc = (), []
    for part in range(parts):
        others = (sibling[part], near[part], near_sibling[part])
        *held, m = cotangent(
            part, parts, tile, preds[part], others, target, area, var, held, members, 1.0 / (points_all * n_vars), pair_coef
        )
        misc.append(m)
    cot, turned = held
    dpre_sib, blocks_sib = backward(1 - core, place_sib, cot, turned, sp, hid, w_padded, lat_t, misc, scale)
    dpre_own, blocks_own = backward(core, place_own, cot, turned, sp, hid, w_padded, lat_t, misc, scale)
    out_own, out_sib = grad_sum(blocks_own, blocks_sib)
    latent_grad = latent_gradient(core, dpre_own, dpre_sib, w_hidden)
    grad_w_hidden, grad_w_output, grad_b_hidden, last = join(core, place_own, place_sib, out_own, out_sib, n_vars)
    return (
        last[0, n_vars],
        grad_w_hidden,
        grad_b_hidden[0],
        grad_w_output,
        last[0, :n_vars],
        latent_grad,
    )


def solution(mesh):
    fine = Mesh(mesh.devices.reshape(2, 2, 2, 4, 4), ALL)
    member, space = ("ylo", "core"), ("yhi", "z", "x")
    return jax.shard_map(
        shards,
        mesh=fine,
        in_specs=(P(member, space, None), P(None, space), P(space), P(), P(), P(), P(), P()),
        out_specs=(P(), P(), P(), P(), P(), P(member, space, None)),
        check_vma=False,
    )
```

```python
import functools
import math

import jax
import jax.numpy as jnp
from jax import lax
from jax.experimental import pallas as pl
from jax.experimental.pallas import tpu as pltpu
from jax.sharding import Mesh, PartitionSpec as P

DELTA = 0.05
ALL = ("ylo", "core", "yhi", "z", "x")
MIB = 1 << 20
F32, BF16 = jnp.float32, jnp.bfloat16


def flat(core, x, y, z):
    return ((y % 2) * 2 + core) * 32 + (y // 2) * 16 + z * 4 + x


def moved(where):
    pairs = []
    for core in range(2):
        for x in range(4):
            for y in range(4):
                for z in range(4):
                    pairs.append((flat(core, x, y, z), flat(*where(core, x, y, z))))
    return pairs


SWAP = moved(lambda c, x, y, z: (1 - c, x, y, z))
NEAR = moved(lambda c, x, y, z: (c, x, y ^ 1, z))


def first(k):
    return moved(lambda c, x, y, z: (c, x, y, (z + k) % 4) if c == 0 else (c, (x + k) % 4, y, z))


def second(k):
    return moved(lambda c, x, y, z: (c, x, y, (z + k) % 4) if c == 1 else (c, (x + k) % 4, y, z))


def along_y(k):
    return moved(lambda c, x, y, z: (c, x, (y + k) % 4, z))


def send(array, pairs):
    return lax.ppermute(array, ALL, pairs)


def grad_sum(own, sibling, beside, dpre):
    core, x, z = lax.axis_index("core"), lax.axis_index("x"), lax.axis_index("z")
    place = jnp.where(core == 0, x, z)
    got = send(sibling, SWAP)
    held = [own[k] + got[k] for k in range(4)]
    held, dpre = lax.optimization_barrier((held, dpre))
    aside = beside(dpre)
    came = [send(held[k], first(k)) for k in (1, 3, 2)]
    *came, aside = lax.optimization_barrier((*came, aside))
    block = held[0] + came[0] + came[1] + came[2]
    rows = block.shape[0] // 4
    quarters = block.reshape((4, rows) + block.shape[1:])
    pick = lambda k: lax.dynamic_index_in_dim(quarters, (place + k) % 4, 0, keepdims=False)
    quarter = pick(0)
    for k in (1, 3, 2):
        quarter = quarter + send(pick(k), second(k))
    quarter = quarter + send(quarter, along_y(1)) + send(quarter, along_y(3)) + send(quarter, along_y(2))
    came = [quarter] + [send(quarter, second(k)) for k in (1, 2, 3)]
    twice = jnp.concatenate([came[3], came[2], came[1], came[0], came[3], came[2], came[1]], 0)
    block = lax.dynamic_slice_in_dim(twice, ((3 - place) % 4) * rows, 4 * rows, 0)
    mine = [block] + [send(block, first(k)) for k in (1, 2, 3)]
    return mine, [send(m, SWAP) for m in mine], aside


def params(mib=56):
    return pltpu.CompilerParams(vmem_limit_bytes=mib * MIB)


def cost(flops, moved_bytes, trans=0):
    return pl.CostEstimate(flops=flops, bytes_accessed=moved_bytes, transcendentals=trans)


def forward_kernel(lat, w, b_hid, w_out, b_out, *refs):
    pred, hid, slope_out = refs[-3:]
    cols = 256
    turned = b_out[...]
    for j in range(0, w.shape[1], cols):
        at = slice(j, j + cols)
        pre = jnp.dot(lat[...], w[:, at], preferred_element_type=F32) + b_hid[:, at]
        sig = jax.nn.sigmoid(pre)
        h = (pre * sig).astype(BF16)
        hid[:, at] = h
        slope_out[:, at] = sig * (1.0 + pre * (1.0 - sig))
        turned = turned + lax.dot_general(h, w_out[:, at], (((1,), (1,)), ((), ())), preferred_element_type=F32)
    pred[...] = jnp.transpose(turned)


def forward(part, n, latent, w_hidden, b_hidden, w_output, b_output, tile=512):
    depth = latent.shape[1]
    width, n_vars = w_hidden.shape[1], w_output.shape[0]
    steps = n // tile
    whole = lambda shape: pl.BlockSpec(shape, lambda g: (0, 0))
    rows = pl.BlockSpec((tile, width), lambda g: (g, 0))
    return pl.pallas_call(
        forward_kernel,
        grid=(steps,),
        in_specs=[
            pl.BlockSpec((tile, depth), lambda g: (part * steps + g, 0)),
            whole(w_hidden.shape),
            whole((1, width)),
            whole(w_output.shape),
            whole((1, n_vars)),
        ],
        out_specs=[pl.BlockSpec((n_vars, tile), lambda g: (0, g)), rows, rows],
        out_shape=[
            jax.ShapeDtypeStruct((n_vars, n), F32),
            jax.ShapeDtypeStruct((n, width), BF16),
            jax.ShapeDtypeStruct((n, width), F32),
        ],
        compiler_params=params(),
        cost_estimate=cost(2 * n * width * (depth + n_vars), n * (2 * depth + 6 * width) + 2 * depth * width, 2 * n * width),
    )(latent, w_hidden, b_hidden.reshape(1, width), w_output, b_output.reshape(1, n_vars))


def cot_kernel(members, scale, loss_scale, pair_coef, own, o1, o2, o3, target, area, var, sp, hid, w_out, *refs):
    dpre, rest, cot_held = refs[-3:]
    n_vars, n = own.shape
    j = pl.program_id(0)
    rest[...] = refs[0][...] if len(refs) > 3 else jnp.zeros_like(rest)

    @pl.when(j == 0)
    def _():
        weights = var[...] * area[...]
        mine = own[...]

        def both(diff):
            u = diff * diff + DELTA * DELTA
            r = lax.rsqrt(u)
            return u * r - DELTA, diff * r

        mag, slo = both(mine - target[...])
        pair_mag, pair_slo = jnp.zeros_like(mine), jnp.zeros_like(mine)
        for other in (o1, o2, o3):
            m, s = both(mine - other[...])
            pair_mag, pair_slo = pair_mag + m, pair_slo + s
        term = weights * (mag * (1.0 / members) - (0.5 * pair_coef) * pair_mag)
        cot = (weights * (slo * (1.0 / members) - pair_coef * pair_slo)).astype(BF16)
        cot_held[...] = cot
        sums = lax.dot_general(
            jnp.ones((16, n), BF16), cot, (((1,), (1,)), ((), ())), preferred_element_type=F32
        )[0:1]
        rest[n_vars + 1 : n_vars + 2, 0:n_vars] += sums * scale
        rest[n_vars + 2 : n_vars + 3, 0:128] += jnp.full((1, 128), jnp.sum(term) * loss_scale, F32)

    cot = cot_held[...]
    back = lax.dot_general(cot, w_out[...], (((0,), (0,)), ((), ())), preferred_element_type=F32)
    d = (back * sp[...]).astype(BF16)
    dpre[...] = d
    rest[0:n_vars, :] += jnp.dot(cot, hid[...], preferred_element_type=F32) * scale
    rest[n_vars : n_vars + 1, :] += jnp.sum(d.astype(F32), axis=0, keepdims=True) * scale


def cotangent(part, n, own, others, target, area, var, sp, hid, w_output, held, members, scale, loss_scale, pair_coef, cols=256):
    n_vars, width = target.shape[0], sp.shape[1]
    local = pl.BlockSpec((n_vars, n), lambda j: (0, 0))
    block = pl.BlockSpec((n, cols), lambda j: (0, j))
    rest = pl.BlockSpec((128, cols), lambda j: (0, j))
    return pl.pallas_call(
        functools.partial(cot_kernel, members, scale, loss_scale, pair_coef),
        grid=(width // cols,),
        in_specs=[local] * 4
        + [
            pl.BlockSpec((n_vars, n), lambda j: (0, part)),
            pl.BlockSpec((1, n), lambda j: (0, part)),
            pl.BlockSpec((n_vars, 1), lambda j: (0, 0)),
            block,
            block,
            pl.BlockSpec((n_vars, cols), lambda j: (0, j)),
        ]
        + [rest] * len(held),
        out_specs=[block, rest],
        out_shape=[
            jax.ShapeDtypeStruct((n, width), BF16),
            jax.ShapeDtypeStruct((128, width), F32),
        ],
        scratch_shapes=[pltpu.VMEM((n_vars, n), BF16)],
        compiler_params=params(),
        cost_estimate=cost(4 * n * n_vars * width, n * (n_vars * 20 + 8 * width), 4 * n * n_vars),
    )(own, *others, target, area, var, sp, hid, w_output, *held)


def weight_kernel(scale, where, lat0, lat1, dpre0, dpre1, rest, out):
    rows, n = lat0.shape[1], dpre0.shape[0]
    dims = (((0,), (0,)), ((), ()))
    for j, lat in enumerate((lat0, lat1)):
        block = lax.rem(where[1] + 2 * pl.program_id(0) + j, 4)
        out[j, 0:rows, :] = (
            lax.dot_general(lat[0:n, :], dpre0[...], dims, preferred_element_type=F32)
            + lax.dot_general(lat[n : 2 * n, :], dpre1[...], dims, preferred_element_type=F32)
        ) * scale
        out[j, rows : rows + 32, :] = rest[pl.ds(pl.multiple_of(block * 32, 32), 32), :]


def weight_grad(which, place, latent, dpre, rest, scale):
    (points, depth), width = latent.shape, dpre[0].shape[1]
    half, rows = width // 2, depth // 4
    halves = pl.BlockSpec((points // 2, half), lambda g, s: (0, s[0]))
    lat = lambda j: pl.BlockSpec((points, rows), lambda g, s: (0, lax.rem(s[1] + 2 * g + j, 4)))
    return pl.pallas_call(
        functools.partial(weight_kernel, scale),
        grid_spec=pltpu.PrefetchScalarGridSpec(
            num_scalar_prefetch=1,
            grid=(2,),
            in_specs=[
                lat(0),
                lat(1),
                halves,
                halves,
                pl.BlockSpec((128, half), lambda g, s: (0, s[0])),
            ],
            out_specs=pl.BlockSpec((2, rows + 32, half), lambda g, s: (g, 0, 0)),
        ),
        out_shape=jax.ShapeDtypeStruct((4, rows + 32, half), F32),
        compiler_params=params(),
        cost_estimate=cost(2 * points * half * depth, points * (2 * half + 2 * depth) + 4 * depth * half),
    )(jnp.stack([which, place]).astype(jnp.int32), latent, latent, *dpre, rest)


def latent_kernel(steps, dpre0, dpre1, w, out):
    g = pl.program_id(0)
    for part, dpre in enumerate((dpre0, dpre1)):

        @pl.when(g // steps == part)
        def _():
            out[0] = lax.dot_general(
                dpre[...], w[...], (((1,), (1,)), ((), ())), preferred_element_type=F32
            ).astype(BF16)


def latent_gradient(dpre, w_hidden, tile=512):
    n, width = dpre[0].shape
    depth, points, steps = w_hidden.shape[0], 2 * n, n // tile
    return pl.pallas_call(
        functools.partial(latent_kernel, steps),
        grid=(2 * steps,),
        in_specs=[
            pl.BlockSpec((tile, width), lambda g: (jnp.minimum(g, steps - 1), 0)),
            pl.BlockSpec((tile, width), lambda g: (jnp.maximum(g - steps, 0), 0)),
            pl.BlockSpec((depth, width), lambda g: (0, 0)),
        ],
        out_specs=pl.BlockSpec((1, tile, depth), lambda g: (0, g, 0)),
        out_shape=jax.ShapeDtypeStruct((1, points, depth), BF16),
        compiler_params=params(),
        cost_estimate=cost(2 * points * width * depth, points * (2 * width + 2 * depth) + 2 * depth * width),
    )(*dpre, w_hidden)


def join_kernel(n_vars, where, *refs):
    ins, (grad_w, grad_o, grad_b, grad_b_out, loss, rest) = refs[:8], refs[8:]
    rows, half = ins[0].shape[0] - 32, ins[0].shape[1]
    for which in range(2):
        col = where[0] if which == 0 else 1 - where[0]
        cols = pl.ds(pl.multiple_of(col * half, half), half)
        for k in range(4):
            block = lax.rem(where[1 + which] - k + 4, 4)
            grad_w[pl.ds(pl.multiple_of(block * rows, rows), rows), cols] = ins[4 * which + k][0:rows, :]
            rest[pl.ds(pl.multiple_of(block * 32, 32), 32), cols] = ins[4 * which + k][rows : rows + 32, :]
    grad_o[...] = rest[0:n_vars, :]
    grad_b[...] = rest[n_vars : n_vars + 1, :]
    grad_b_out[...] = rest[n_vars + 1 : n_vars + 2, 0:n_vars]
    loss[...] = rest[n_vars + 2 : n_vars + 3, 0:1]


def join(where, own, sib, n_vars):
    rows, half = own[0].shape
    depth, width = 4 * (rows - 32), 2 * half
    vmem = pl.BlockSpec(memory_space=pltpu.VMEM)
    return pl.pallas_call(
        functools.partial(join_kernel, n_vars),
        in_specs=[pl.BlockSpec(memory_space=pltpu.SMEM)] + [vmem] * 8,
        out_specs=[vmem] * 5,
        out_shape=[
            jax.ShapeDtypeStruct((depth, width), F32),
            jax.ShapeDtypeStruct((n_vars, width), F32),
            jax.ShapeDtypeStruct((1, width), F32),
            jax.ShapeDtypeStruct((1, n_vars), F32),
            jax.ShapeDtypeStruct((1, 1), F32),
        ],
        scratch_shapes=[pltpu.VMEM((128, width), F32)],
        compiler_params=params(16),
        cost_estimate=cost(0, 8 * depth * width),
    )(where, *own, *sib)


def shards(latent, target, area_weight, var_weight, w_hidden, b_hidden, w_output, b_output):
    members = 4
    parts = [(0, 1024), (1, 1024)]
    n_vars, points = target.shape
    points_all = points * 32
    eps = 0.05 / members
    pair_coef = (1.0 - eps) / (members * (members - 1))
    scale = 1.0 / math.sqrt(members * points_all)
    loss_scale = 1.0 / (points_all * n_vars)
    core, x, z = lax.axis_index("core"), lax.axis_index("x"), lax.axis_index("z")
    place_own = jnp.where(core == 0, z, x)
    place_sib = jnp.where(core == 0, x, z)
    own_latent = latent[0]
    made = [forward(part, n, own_latent, w_hidden, b_hidden, w_output, b_output) for part, n in parts]
    area, var = area_weight.reshape(1, points), var_weight.reshape(n_vars, 1)
    dpre, rest, after = [], (), made[-1][0]
    for (part, n), (pred, hid, sp) in zip(parts, made):
        near = send(pred, NEAR)
        near, after = lax.optimization_barrier((near, after))
        others = (send(pred, SWAP), near, send(near, SWAP))
        d, total = cotangent(
            part, n, pred, others, target, area, var, sp, hid, w_output, rest, members, scale, loss_scale, pair_coef
        )
        dpre.append(d)
        rest, after = (total,), total
    rest = after
    blocks_sib = weight_grad(1 - core, place_sib, own_latent, dpre, rest, scale)
    blocks_own = weight_grad(core, place_own, own_latent, dpre, rest, scale)
    out_own, out_sib, latent_grad = grad_sum(blocks_own, blocks_sib, lambda d: latent_gradient(d, w_hidden), dpre)
    where = jnp.stack([core, place_own, place_sib]).astype(jnp.int32)
    grad_w_hidden, grad_w_output, grad_b_hidden, grad_b_output, loss = join(where, out_own, out_sib, n_vars)
    return (
        loss.reshape(()),
        grad_w_hidden,
        grad_b_hidden.reshape(-1),
        grad_w_output,
        grad_b_output.reshape(-1),
        latent_grad,
    )


def solution(mesh):
    fine = Mesh(mesh.devices.reshape(2, 2, 2, 4, 4), ALL)
    member, space = ("ylo", "core"), ("yhi", "z", "x")
    return jax.shard_map(
        shards,
        mesh=fine,
        in_specs=(P(member, space, None), P(None, space), P(space), P(), P(), P(), P(), P()),
        out_specs=(P(), P(), P(), P(), P(), P(member, space, None)),
        check_vma=False,
    )
```

```python
import functools
import math

import jax
import jax.numpy as jnp
from jax import lax
from jax.experimental import pallas as pl
from jax.experimental.pallas import tpu as pltpu
from jax.sharding import Mesh, PartitionSpec as P

DELTA = 0.05
ALL = ("ylo", "core", "yhi", "z", "x")
MIB = 1 << 20
F32, BF16 = jnp.float32, jnp.bfloat16


def flat(core, x, y, z):
    return ((y % 2) * 2 + core) * 32 + (y // 2) * 16 + z * 4 + x


def moved(where):
    pairs = []
    for core in range(2):
        for x in range(4):
            for y in range(4):
                for z in range(4):
                    pairs.append((flat(core, x, y, z), flat(*where(core, x, y, z))))
    return pairs


SWAP = moved(lambda c, x, y, z: (1 - c, x, y, z))
NEAR = moved(lambda c, x, y, z: (c, x, y ^ 1, z))


def first(k):
    return moved(lambda c, x, y, z: (c, x, y, (z + k) % 4) if c == 0 else (c, (x + k) % 4, y, z))


def second(k):
    return moved(lambda c, x, y, z: (c, x, y, (z + k) % 4) if c == 1 else (c, (x + k) % 4, y, z))


def along_y(k):
    return moved(lambda c, x, y, z: (c, x, (y + k) % 4, z))


def send(array, pairs):
    return lax.ppermute(array, ALL, pairs)


def grad_sum(own, sibling, beside, dpre):
    core, x, z = lax.axis_index("core"), lax.axis_index("x"), lax.axis_index("z")
    place = jnp.where(core == 0, x, z)
    got = send(sibling, SWAP)
    held = {}
    for k in (2, 1, 3, 0):
        held[k], own, got = lax.optimization_barrier((own[k] + got[k], own, got))
    kept, dpre = lax.optimization_barrier((held[0], dpre))
    aside = beside(dpre)
    came = [send(held[k], first(k)) for k in (2, 1, 3)]
    came, aside = lax.optimization_barrier((came, aside))
    block = kept + came[0] + came[1] + came[2]
    rows = block.shape[0] // 4
    quarters = block.reshape((4, rows) + block.shape[1:])
    pick = lambda k: lax.dynamic_index_in_dim(quarters, (place + k) % 4, 0, keepdims=False)
    quarter = pick(0)
    for k in (1, 3, 2):
        quarter = quarter + send(pick(k), second(k))
    quarter = quarter + send(quarter, along_y(1)) + send(quarter, along_y(3)) + send(quarter, along_y(2))
    came = [quarter] + [send(quarter, second(k)) for k in (1, 2, 3)]
    twice = jnp.concatenate([came[3], came[2], came[1], came[0], came[3], came[2], came[1]], 0)
    block = lax.dynamic_slice_in_dim(twice, ((3 - place) % 4) * rows, 4 * rows, 0)
    mine = [block] + [send(block, first(k)) for k in (1, 2, 3)]
    return mine, [send(m, SWAP) for m in mine], aside


def params(mib=56):
    return pltpu.CompilerParams(vmem_limit_bytes=mib * MIB)


def cost(flops, moved_bytes, trans=0):
    return pl.CostEstimate(flops=flops, bytes_accessed=moved_bytes, transcendentals=trans)


def forward_kernel(lat, w, b_hid, w_out, b_out, pred, hid, slope_out):
    cols = 256
    for j in range(0, w.shape[1], cols):
        at = slice(j, j + cols)
        pre = jnp.dot(lat[...], w[:, at], preferred_element_type=F32) + b_hid[:, at]
        sig = jax.nn.sigmoid(pre)
        hid[:, at] = (pre * sig).astype(BF16)
        slope_out[:, at] = sig * (1.0 + pre * (1.0 - sig))
    n_vars = w_out.shape[0]
    bias = jnp.transpose(jnp.broadcast_to(b_out[...], (128, n_vars)))[:, 0:1]
    pred[...] = bias + lax.dot_general(w_out[...], hid[...], (((1,), (1,)), ((), ())), preferred_element_type=F32)


def forward(part, n, latent, w_hidden, b_hidden, w_output, b_output, tile=512):
    depth = latent.shape[1]
    width, n_vars = w_hidden.shape[1], w_output.shape[0]
    steps = n // tile
    whole = lambda shape: pl.BlockSpec(shape, lambda g: (0, 0))
    rows = pl.BlockSpec((tile, width), lambda g: (g, 0))
    return pl.pallas_call(
        forward_kernel,
        grid=(steps,),
        in_specs=[
            pl.BlockSpec((tile, depth), lambda g: (part * steps + g, 0)),
            whole(w_hidden.shape),
            whole((1, width)),
            whole(w_output.shape),
            whole((1, n_vars)),
        ],
        out_specs=[pl.BlockSpec((n_vars, tile), lambda g: (0, g)), rows, rows],
        out_shape=[
            jax.ShapeDtypeStruct((n_vars, n), F32),
            jax.ShapeDtypeStruct((n, width), BF16),
            jax.ShapeDtypeStruct((n, width), F32),
        ],
        compiler_params=params(),
        cost_estimate=cost(2 * n * width * (depth + n_vars), n * (2 * depth + 6 * width) + 2 * depth * width, 2 * n * width),
    )(latent, w_hidden, b_hidden.reshape(1, width), w_output, b_output.reshape(1, n_vars))


def cot_tile(members, scale, loss_scale, pair_coef, own, o1, o2, o3, target, area, var, sp, hid, w_out, rest):
    n_vars, n = own.shape
    weights = var[...] * area[...]
    mine = own[...]

    def both(diff):
        u = diff * diff + DELTA * DELTA
        r = lax.rsqrt(u)
        return u * r - DELTA, diff * r

    mag, slo = both(mine - target[...])
    pair_mag, pair_slo = jnp.zeros_like(mine), jnp.zeros_like(mine)
    for other in (o1, o2, o3):
        m, s = both(mine - other[...])
        pair_mag, pair_slo = pair_mag + m, pair_slo + s
    term = weights * (mag * (1.0 / members) - (0.5 * pair_coef) * pair_mag)
    cot = (weights * (slo * (1.0 / members) - pair_coef * pair_slo)).astype(BF16)
    sums = lax.dot_general(
        jnp.ones((16, n), BF16), cot, (((1,), (1,)), ((), ())), preferred_element_type=F32
    )[0:1]
    rest[n_vars + 1 : n_vars + 2, 0:n_vars] += sums * scale
    rest[n_vars + 2 : n_vars + 3, 0:128] += jnp.full((1, 128), jnp.sum(term) * loss_scale, F32)

    back = lax.dot_general(cot, w_out[...], (((0,), (0,)), ((), ())), preferred_element_type=F32)
    d = (back * sp[...]).astype(BF16)
    rest[0:n_vars, :] += jnp.dot(cot, hid[...], preferred_element_type=F32) * scale
    rest[n_vars : n_vars + 1, :] += jnp.sum(d.astype(F32), axis=0, keepdims=True) * scale
    return d


def cot_kernel(numbers, *refs):
    dpre, rest = refs[-2:]

    @pl.when(pl.program_id(0) == 0)
    def _():
        rest[...] = jnp.zeros_like(rest)

    dpre[...] = cot_tile(*numbers, *refs[:10], rest)


def weight_blocks(scale, which, where, step, lats, dpres, rest, out):
    rows, half = lats[0].shape[1], out.shape[2]
    for j, lat in enumerate(lats):
        total, start = 0.0, 0
        for d in dpres:
            n = d.shape[0]
            total += lax.dot_general(
                lat[start : start + n, :], d, (((0,), (0,)), ((), ())), preferred_element_type=F32
            )
            start += n
        block = lax.rem(where[2 + which] + 2 * step + j, 4)
        out[j, 0:rows, :] = total * scale
        cols = pl.ds(pl.multiple_of(where[which] * half, half), half)
        out[j, rows : rows + 32, :] = rest[pl.ds(pl.multiple_of(block * 32, 32), 32), cols]


def cot_weight_kernel(numbers, steps, which, where, *refs):
    ins, (rest_in, lat0, lat1, dpre0), (dpre, rest, out, held) = refs[:10], refs[10:14], refs[14:]
    g = pl.program_id(0)
    tile, half = dpre.shape[0], out.shape[2]

    @pl.when(g == 0)
    def _():
        rest[...] = rest_in[...]

    @pl.when(g < steps)
    def _():
        d = cot_tile(*numbers, *ins, rest)
        dpre[...] = d
        held[pl.ds(pl.multiple_of(g * tile, tile), tile), :] = d

    @pl.when(g >= steps)
    def _():
        cols = pl.ds(pl.multiple_of(where[which] * half, half), half)
        weight_blocks(numbers[1], which, where, g - steps, (lat0, lat1), (dpre0[...], held[:, cols]), rest, out)


def cotangent(numbers, part, own, others, target, area, var, sp, hid, w_output, tile=512):
    n, width = sp.shape
    n_vars, steps = target.shape[0], n // tile
    whole = lambda shape: pl.BlockSpec(shape, lambda g: (0, 0))
    local = pl.BlockSpec((n_vars, tile), lambda g: (0, g))
    rows = pl.BlockSpec((tile, width), lambda g: (g, 0))
    return pl.pallas_call(
        functools.partial(cot_kernel, numbers),
        grid=(steps,),
        in_specs=[local] * 4
        + [
            pl.BlockSpec((n_vars, tile), lambda g: (0, part * steps + g)),
            pl.BlockSpec((1, tile), lambda g: (0, part * steps + g)),
            whole((n_vars, 1)),
            rows,
            rows,
            whole(w_output.shape),
        ],
        out_specs=[rows, whole((128, width))],
        out_shape=[
            jax.ShapeDtypeStruct((n, width), BF16),
            jax.ShapeDtypeStruct((128, width), F32),
        ],
        compiler_params=params(),
        cost_estimate=cost(1, 1),
    )(own, *others, target, area, var, sp, hid, w_output)


def cotangent_weight(
    numbers, part, which, where, own, others, target, area, var, sp, hid, w_output, rest, latent, dpre0, tile=512
):
    n, width = sp.shape
    points, depth = latent.shape
    n_vars, steps, half, block = target.shape[0], n // tile, width // 2, depth // 4
    at = lambda g: jnp.minimum(g, steps - 1)
    step = lambda g: jnp.maximum(g - steps, 0)
    whole = lambda shape: pl.BlockSpec(shape, lambda g, s: (0, 0))
    local = pl.BlockSpec((n_vars, tile), lambda g, s: (0, at(g)))
    rows = pl.BlockSpec((tile, width), lambda g, s: (at(g), 0))
    lat = lambda j: pl.BlockSpec((points, block), lambda g, s: (0, lax.rem(s[2 + which] + 2 * step(g) + j, 4)))
    return pl.pallas_call(
        functools.partial(cot_weight_kernel, numbers, steps, which),
        grid_spec=pltpu.PrefetchScalarGridSpec(
            num_scalar_prefetch=1,
            grid=(steps + 2,),
            in_specs=[local] * 4
            + [
                pl.BlockSpec((n_vars, tile), lambda g, s: (0, part * steps + at(g))),
                pl.BlockSpec((1, tile), lambda g, s: (0, part * steps + at(g))),
                whole((n_vars, 1)),
                rows,
                rows,
                whole(w_output.shape),
                whole((128, width)),
                lat(0),
                lat(1),
                pl.BlockSpec((n, half), lambda g, s: (0, s[which])),
            ],
            out_specs=[rows, whole((128, width)), pl.BlockSpec((2, block + 32, half), lambda g, s: (step(g), 0, 0))],
            scratch_shapes=[pltpu.VMEM((n, width), BF16)],
        ),
        out_shape=[
            jax.ShapeDtypeStruct((n, width), BF16),
            jax.ShapeDtypeStruct((128, width), F32),
            jax.ShapeDtypeStruct((4, block + 32, half), F32),
        ],
        compiler_params=params(),
        cost_estimate=cost(2 * points * half * depth, points * 2 * depth + n * (n_vars * 20 + 8 * width) + 4 * depth * half),
    )(where, own, *others, target, area, var, sp, hid, w_output, rest, latent, latent, dpre0)


def weight_kernel(scale, which, where, lat0, lat1, dpre0, dpre1, rest, out):
    weight_blocks(scale, which, where, pl.program_id(0), (lat0, lat1), (dpre0[...], dpre1[...]), rest, out)


def weight_grad(which, where, latent, dpre, rest, scale):
    (points, depth), width = latent.shape, dpre[0].shape[1]
    half, rows = width // 2, depth // 4
    halves = pl.BlockSpec((points // 2, half), lambda g, s: (0, s[which]))
    lat = lambda j: pl.BlockSpec((points, rows), lambda g, s: (0, lax.rem(s[2 + which] + 2 * g + j, 4)))
    return pl.pallas_call(
        functools.partial(weight_kernel, scale, which),
        grid_spec=pltpu.PrefetchScalarGridSpec(
            num_scalar_prefetch=1,
            grid=(2,),
            in_specs=[
                lat(0),
                lat(1),
                halves,
                halves,
                pl.BlockSpec((128, width), lambda g, s: (0, 0)),
            ],
            out_specs=pl.BlockSpec((2, rows + 32, half), lambda g, s: (g, 0, 0)),
        ),
        out_shape=jax.ShapeDtypeStruct((4, rows + 32, half), F32),
        compiler_params=params(),
        cost_estimate=cost(2 * points * half * depth, points * (2 * half + 2 * depth) + 4 * depth * half),
    )(where, latent, latent, *dpre, rest)


def latent_kernel(steps, dpre0, dpre1, w, out):
    g = pl.program_id(0)
    for part, dpre in enumerate((dpre0, dpre1)):

        @pl.when(g // steps == part)
        def _():
            out[0] = lax.dot_general(
                dpre[...], w[...], (((1,), (1,)), ((), ())), preferred_element_type=F32
            ).astype(BF16)


def latent_gradient(dpre, w_hidden, tile=512):
    n, width = dpre[0].shape
    depth, points, steps = w_hidden.shape[0], 2 * n, n // tile
    return pl.pallas_call(
        functools.partial(latent_kernel, steps),
        grid=(2 * steps,),
        in_specs=[
            pl.BlockSpec((tile, width), lambda g: (jnp.minimum(g, steps - 1), 0)),
            pl.BlockSpec((tile, width), lambda g: (jnp.maximum(g - steps, 0), 0)),
            pl.BlockSpec((depth, width), lambda g: (0, 0)),
        ],
        out_specs=pl.BlockSpec((1, tile, depth), lambda g: (0, g, 0)),
        out_shape=jax.ShapeDtypeStruct((1, points, depth), BF16),
        compiler_params=params(),
        cost_estimate=cost(2 * points * width * depth, points * (2 * width + 2 * depth) + 2 * depth * width),
    )(*dpre, w_hidden)


def join_kernel(n_vars, where, *refs):
    ins, (grad_w, grad_o, grad_b, grad_b_out, loss, rest) = refs[:8], refs[8:]
    rows, half = ins[0].shape[0] - 32, ins[0].shape[1]
    for which in range(2):
        cols = pl.ds(pl.multiple_of(where[which] * half, half), half)
        for k in range(4):
            block = lax.rem(where[2 + which] - k + 4, 4)
            grad_w[pl.ds(pl.multiple_of(block * rows, rows), rows), cols] = ins[4 * which + k][0:rows, :]
            rest[pl.ds(pl.multiple_of(block * 32, 32), 32), cols] = ins[4 * which + k][rows : rows + 32, :]
    grad_o[...] = rest[0:n_vars, :]
    grad_b[...] = rest[n_vars : n_vars + 1, :]
    grad_b_out[...] = rest[n_vars + 1 : n_vars + 2, 0:n_vars]
    loss[...] = rest[n_vars + 2 : n_vars + 3, 0:1]


def join(where, own, sib, n_vars):
    rows, half = own[0].shape
    depth, width = 4 * (rows - 32), 2 * half
    vmem = pl.BlockSpec(memory_space=pltpu.VMEM)
    return pl.pallas_call(
        functools.partial(join_kernel, n_vars),
        in_specs=[pl.BlockSpec(memory_space=pltpu.SMEM)] + [vmem] * 8,
        out_specs=[vmem] * 5,
        out_shape=[
            jax.ShapeDtypeStruct((depth, width), F32),
            jax.ShapeDtypeStruct((n_vars, width), F32),
            jax.ShapeDtypeStruct((1, width), F32),
            jax.ShapeDtypeStruct((1, n_vars), F32),
            jax.ShapeDtypeStruct((1, 1), F32),
        ],
        scratch_shapes=[pltpu.VMEM((128, width), F32)],
        compiler_params=params(16),
        cost_estimate=cost(0, 8 * depth * width),
    )(where, *own, *sib)


def shards(latent, target, area_weight, var_weight, w_hidden, b_hidden, w_output, b_output):
    members = 4
    parts = [(0, 1024), (1, 1024)]
    n_vars, points = target.shape
    points_all = points * 32
    eps = 0.05 / members
    pair_coef = (1.0 - eps) / (members * (members - 1))
    scale = 1.0 / math.sqrt(members * points_all)
    loss_scale = 1.0 / (points_all * n_vars)
    core, x, z = lax.axis_index("core"), lax.axis_index("x"), lax.axis_index("z")
    place_own = jnp.where(core == 0, z, x)
    place_sib = jnp.where(core == 0, x, z)
    where = jnp.stack([core, 1 - core, place_own, place_sib]).astype(jnp.int32)
    own_latent = latent[0]
    made = [forward(part, n, own_latent, w_hidden, b_hidden, w_output, b_output) for part, n in parts]
    area, var = area_weight.reshape(1, points), var_weight.reshape(n_vars, 1)
    numbers = (members, scale, loss_scale, pair_coef)

    (pred0, hid0, sp0), (pred1, hid1, sp1) = made
    near0, near1 = send(pred0, NEAR), send(pred1, NEAR)
    sib0, sib1 = send(pred0, SWAP), send(pred1, SWAP)
    near0, sib0, sib1, where = lax.optimization_barrier((near0, sib0, sib1, where))
    others = (sib0, near0, send(near0, SWAP))
    dpre0, rest = cotangent(numbers, 0, pred0, others, target, area, var, sp0, hid0, w_output)
    near1, rest = lax.optimization_barrier((near1, rest))
    others = (sib1, near1, send(near1, SWAP))
    dpre1, rest, blocks_sib = cotangent_weight(
        numbers, 1, 1, where, pred1, others, target, area, var, sp1, hid1, w_output, rest, own_latent, dpre0
    )
    dpre = (dpre0, dpre1)
    blocks_own = weight_grad(0, where, own_latent, dpre, rest, scale)
    out_own, out_sib, latent_grad = grad_sum(blocks_own, blocks_sib, lambda d: latent_gradient(d, w_hidden), dpre)
    grad_w_hidden, grad_w_output, grad_b_hidden, grad_b_output, loss = join(where, out_own, out_sib, n_vars)
    return (
        loss.reshape(()),
        grad_w_hidden,
        grad_b_hidden.reshape(-1),
        grad_w_output,
        grad_b_output.reshape(-1),
        latent_grad,
    )


def solution(mesh):
    fine = Mesh(mesh.devices.reshape(2, 2, 2, 4, 4), ALL)
    member, space = ("ylo", "core"), ("yhi", "z", "x")
    return jax.shard_map(
        shards,
        mesh=fine,
        in_specs=(P(member, space, None), P(None, space), P(space), P(), P(), P(), P(), P()),
        out_specs=(P(), P(), P(), P(), P(), P(member, space, None)),
        check_vma=False,
    )
```

```python
import functools
import math

import jax
import jax.numpy as jnp
from jax import lax
from jax.experimental import pallas as pl
from jax.experimental.pallas import tpu as pltpu
from jax.sharding import Mesh, PartitionSpec as P

DELTA = 0.05
ALL = ("ylo", "core", "yhi", "z", "x")
MIB = 1 << 20
F32, BF16 = jnp.float32, jnp.bfloat16


def flat(core, x, y, z):
    return ((y % 2) * 2 + core) * 32 + (y // 2) * 16 + z * 4 + x


def moved(where):
    pairs = []
    for core in range(2):
        for x in range(4):
            for y in range(4):
                for z in range(4):
                    pairs.append((flat(core, x, y, z), flat(*where(core, x, y, z))))
    return pairs


SWAP = moved(lambda c, x, y, z: (1 - c, x, y, z))
NEAR = moved(lambda c, x, y, z: (c, x, y ^ 1, z))


def first(k):
    return moved(lambda c, x, y, z: (c, x, y, (z + k) % 4) if c == 0 else (c, (x + k) % 4, y, z))


def second(k):
    return moved(lambda c, x, y, z: (c, x, y, (z + k) % 4) if c == 1 else (c, (x + k) % 4, y, z))


def along_y(k):
    return moved(lambda c, x, y, z: (c, x, (y + k) % 4, z))


def send(array, pairs):
    return lax.ppermute(array, ALL, pairs)


def grad_sum(own, sibling, beside, dpre):
    core, x, z = lax.axis_index("core"), lax.axis_index("x"), lax.axis_index("z")
    place = jnp.where(core == 0, x, z)
    got = send(sibling, SWAP)
    held = {}
    for k in (2, 1, 3, 0):
        held[k], own, got = lax.optimization_barrier((own[k] + got[k], own, got))
    kept, dpre = lax.optimization_barrier((held[0], dpre))
    aside = beside(dpre)
    came = [send(held[k], first(k)) for k in (2, 1, 3)]
    came, aside = lax.optimization_barrier((came, aside))
    block = kept + came[0] + came[1] + came[2]
    rows = block.shape[0] // 4
    quarters = block.reshape((4, rows) + block.shape[1:])
    pick = lambda k: lax.dynamic_index_in_dim(quarters, (place + k) % 4, 0, keepdims=False)
    quarter = pick(0)
    for k in (1, 3, 2):
        quarter = quarter + send(pick(k), second(k))
    quarter = quarter + send(quarter, along_y(1)) + send(quarter, along_y(3)) + send(quarter, along_y(2))
    came = [quarter] + [send(quarter, second(k)) for k in (1, 2, 3)]
    twice = jnp.concatenate([came[3], came[2], came[1], came[0], came[3], came[2], came[1]], 0)
    block = lax.dynamic_slice_in_dim(twice, ((3 - place) % 4) * rows, 4 * rows, 0)
    mine = [block] + [send(block, first(k)) for k in (1, 2, 3)]
    return mine, [send(m, SWAP) for m in mine], aside


def params(mib=56):
    return pltpu.CompilerParams(vmem_limit_bytes=mib * MIB)


def cost(flops, moved_bytes, trans=0):
    return pl.CostEstimate(flops=flops, bytes_accessed=moved_bytes, transcendentals=trans)


def forward_kernel(lat, w, b_hid, w_out, b_out, pred, hid, slope_out):
    cols = 256
    for j in range(0, w.shape[1], cols):
        at = slice(j, j + cols)
        pre = jnp.dot(lat[...], w[:, at], preferred_element_type=F32) + b_hid[:, at]
        sig = jax.nn.sigmoid(pre)
        hid[:, at] = (pre * sig).astype(BF16)
        slope_out[:, at] = sig * (1.0 + pre * (1.0 - sig))
    n_vars = w_out.shape[0]
    bias = jnp.transpose(jnp.broadcast_to(b_out[...], (128, n_vars)))[:, 0:1]
    pred[...] = bias + lax.dot_general(w_out[...], hid[...], (((1,), (1,)), ((), ())), preferred_element_type=F32)


def forward(part, n, latent, w_hidden, b_hidden, w_output, b_output, tile=512):
    depth = latent.shape[1]
    width, n_vars = w_hidden.shape[1], w_output.shape[0]
    steps = n // tile
    whole = lambda shape: pl.BlockSpec(shape, lambda g: (0, 0))
    rows = pl.BlockSpec((tile, width), lambda g: (g, 0))
    return pl.pallas_call(
        forward_kernel,
        grid=(steps,),
        in_specs=[
            pl.BlockSpec((tile, depth), lambda g: (part * steps + g, 0)),
            whole(w_hidden.shape),
            whole((1, width)),
            whole(w_output.shape),
            whole((1, n_vars)),
        ],
        out_specs=[pl.BlockSpec((n_vars, tile), lambda g: (0, g)), rows, rows],
        out_shape=[
            jax.ShapeDtypeStruct((n_vars, n), F32),
            jax.ShapeDtypeStruct((n, width), BF16),
            jax.ShapeDtypeStruct((n, width), F32),
        ],
        compiler_params=params(),
        cost_estimate=cost(2 * n * width * (depth + n_vars), n * (2 * depth + 6 * width) + 2 * depth * width, 2 * n * width),
    )(latent, w_hidden, b_hidden.reshape(1, width), w_output, b_output.reshape(1, n_vars))


def cot_tile(members, scale, loss_scale, pair_coef, own, o1, o2, o3, target, area, var, sp, hid, w_out, rest):
    n_vars, n = own.shape
    weights = var[...] * area[...]
    mine = own[...]

    def both(diff):
        u = diff * diff + DELTA * DELTA
        r = lax.rsqrt(u)
        return u * r - DELTA, diff * r

    mag, slo = both(mine - target[...])
    pair_mag, pair_slo = jnp.zeros_like(mine), jnp.zeros_like(mine)
    for other in (o1, o2, o3):
        m, s = both(mine - other[...])
        pair_mag, pair_slo = pair_mag + m, pair_slo + s
    term = weights * (mag * (1.0 / members) - (0.5 * pair_coef) * pair_mag)
    cot = (weights * (slo * (1.0 / members) - pair_coef * pair_slo)).astype(BF16)
    sums = lax.dot_general(
        jnp.ones((16, n), BF16), cot, (((1,), (1,)), ((), ())), preferred_element_type=F32
    )[0:1]
    rest[n_vars + 1 : n_vars + 2, 0:n_vars] += sums * scale
    rest[n_vars + 2 : n_vars + 3, 0:128] += jnp.full((1, 128), jnp.sum(term) * loss_scale, F32)

    back = lax.dot_general(cot, w_out[...], (((0,), (0,)), ((), ())), preferred_element_type=F32)
    d = (back * sp[...]).astype(BF16)
    rest[0:n_vars, :] += jnp.dot(cot, hid[...], preferred_element_type=F32) * scale
    rest[n_vars : n_vars + 1, :] += jnp.sum(d.astype(F32), axis=0, keepdims=True) * scale
    return d


def cot_kernel(numbers, *refs):
    dpre, rest = refs[-2:]

    @pl.when(pl.program_id(0) == 0)
    def _():
        rest[...] = jnp.zeros_like(rest)

    dpre[...] = cot_tile(*numbers, *refs[:10], rest)


def block_copies(which, where, lat, held, sems, dpre, to):
    rows, half = held.shape[2], to.shape[1]
    cols = pl.ds(pl.multiple_of(where[which] * half, half), half)

    def columns(k):
        block = lax.rem(where[2 + which] + k, 4)
        at = pl.ds(pl.multiple_of(block * rows, rows), rows)
        return pltpu.make_async_copy(lat.at[:, at], held.at[k], sems.at[k])

    return columns, pltpu.make_async_copy(dpre.at[:, cols], to, sems.at[4])


def weight_block(scale, which, where, k, lat, dpres, rest, out, j=0):
    rows, half = lat.shape[1], out.shape[2]
    total, start = 0.0, 0
    for d in dpres:
        n = d.shape[0]
        total += lax.dot_general(lat[start : start + n, :], d, (((0,), (0,)), ((), ())), preferred_element_type=F32)
        start += n
    block = lax.rem(where[2 + which] + k, 4)
    out[j, 0:rows, :] = total * scale
    cols = pl.ds(pl.multiple_of(where[which] * half, half), half)
    out[j, rows : rows + 32, :] = rest[pl.ds(pl.multiple_of(block * 32, 32), 32), cols]


def cot_weight_kernel(numbers, steps, which, where, *refs):
    ins, (rest_in, lat, dpre0), (dpre, rest, out, mine, lat_held, half0, sems) = refs[:10], refs[10:13], refs[13:]
    g = pl.program_id(0)
    tile, half = dpre.shape[0], out.shape[2]
    columns, first_half = block_copies(which, where, lat, lat_held, sems, dpre0, half0)

    @pl.when(g == 0)
    def _():
        first_half.start()
        for k in range(4):
            columns(k).start()
        rest[...] = rest_in[...]

    @pl.when(g < steps)
    def _():
        d = cot_tile(*numbers, *ins, rest)
        dpre[...] = d
        mine[pl.ds(pl.multiple_of(g * tile, tile), tile), :] = d

    @pl.when(g == steps)
    def _():
        first_half.wait()

    @pl.when(g >= steps)
    def _():
        columns(g - steps).wait()
        cols = pl.ds(pl.multiple_of(where[which] * half, half), half)
        weight_block(
            numbers[1], which, where, g - steps, lat_held.at[g - steps], (half0[...], mine[:, cols]), rest, out
        )


def cotangent(numbers, part, own, others, target, area, var, sp, hid, w_output, tile=512):
    n, width = sp.shape
    n_vars, steps = target.shape[0], n // tile
    whole = lambda shape: pl.BlockSpec(shape, lambda g: (0, 0))
    local = pl.BlockSpec((n_vars, tile), lambda g: (0, g))
    rows = pl.BlockSpec((tile, width), lambda g: (g, 0))
    return pl.pallas_call(
        functools.partial(cot_kernel, numbers),
        grid=(steps,),
        in_specs=[local] * 4
        + [
            pl.BlockSpec((n_vars, tile), lambda g: (0, part * steps + g)),
            pl.BlockSpec((1, tile), lambda g: (0, part * steps + g)),
            whole((n_vars, 1)),
            rows,
            rows,
            whole(w_output.shape),
        ],
        out_specs=[rows, whole((128, width))],
        out_shape=[
            jax.ShapeDtypeStruct((n, width), BF16),
            jax.ShapeDtypeStruct((128, width), F32),
        ],
        compiler_params=params(),
        cost_estimate=cost(1, 1),
    )(own, *others, target, area, var, sp, hid, w_output)


def cotangent_weight(
    numbers, part, which, where, own, others, target, area, var, sp, hid, w_output, rest, latent, dpre0, tile=512
):
    n, width = sp.shape
    points, depth = latent.shape
    n_vars, steps, half, block = target.shape[0], n // tile, width // 2, depth // 4
    at = lambda g: jnp.minimum(g, steps - 1)
    step = lambda g: jnp.maximum(g - steps, 0)
    whole = lambda shape: pl.BlockSpec(shape, lambda g, s: (0, 0))
    local = pl.BlockSpec((n_vars, tile), lambda g, s: (0, at(g)))
    rows = pl.BlockSpec((tile, width), lambda g, s: (at(g), 0))
    hbm = pl.BlockSpec(memory_space=pl.ANY)
    return pl.pallas_call(
        functools.partial(cot_weight_kernel, numbers, steps, which),
        grid_spec=pltpu.PrefetchScalarGridSpec(
            num_scalar_prefetch=1,
            grid=(steps + 4,),
            in_specs=[local] * 4
            + [
                pl.BlockSpec((n_vars, tile), lambda g, s: (0, part * steps + at(g))),
                pl.BlockSpec((1, tile), lambda g, s: (0, part * steps + at(g))),
                whole((n_vars, 1)),
                rows,
                rows,
                whole(w_output.shape),
                whole((128, width)),
                hbm,
                hbm,
            ],
            out_specs=[rows, whole((128, width)), pl.BlockSpec((1, block + 32, half), lambda g, s: (step(g), 0, 0))],
            scratch_shapes=[
                pltpu.VMEM((n, width), BF16),
                pltpu.VMEM((4, points, block), BF16),
                pltpu.VMEM((points - n, half), BF16),
                pltpu.SemaphoreType.DMA((5,)),
            ],
        ),
        out_shape=[
            jax.ShapeDtypeStruct((n, width), BF16),
            jax.ShapeDtypeStruct((128, width), F32),
            jax.ShapeDtypeStruct((4, block + 32, half), F32),
        ],
        compiler_params=params(),
        cost_estimate=cost(2 * points * half * depth, points * 2 * depth + n * (n_vars * 20 + 8 * width) + 4 * depth * half),
    )(where, own, *others, target, area, var, sp, hid, w_output, rest, latent, dpre0)


def weight_kernel(scale, which, where, lat0, lat1, dpre0, dpre1, rest, out):
    for j, lat in enumerate((lat0, lat1)):
        weight_block(scale, which, where, 2 * pl.program_id(0) + j, lat, (dpre0[...], dpre1[...]), rest, out, j)


def weight_grad(which, where, latent, dpre, rest, scale):
    (points, depth), width = latent.shape, dpre[0].shape[1]
    half, rows = width // 2, depth // 4
    halves = pl.BlockSpec((points // 2, half), lambda g, s: (0, s[which]))
    lat = lambda j: pl.BlockSpec((points, rows), lambda g, s: (0, lax.rem(s[2 + which] + 2 * g + j, 4)))
    return pl.pallas_call(
        functools.partial(weight_kernel, scale, which),
        grid_spec=pltpu.PrefetchScalarGridSpec(
            num_scalar_prefetch=1,
            grid=(2,),
            in_specs=[
                lat(0),
                lat(1),
                halves,
                halves,
                pl.BlockSpec((128, width), lambda g, s: (0, 0)),
            ],
            out_specs=pl.BlockSpec((2, rows + 32, half), lambda g, s: (g, 0, 0)),
        ),
        out_shape=jax.ShapeDtypeStruct((4, rows + 32, half), F32),
        compiler_params=params(),
        cost_estimate=cost(2 * points * half * depth, points * (2 * half + 2 * depth) + 4 * depth * half),
    )(where, latent, latent, *dpre, rest)


def latent_kernel(steps, dpre0, dpre1, w, out):
    g = pl.program_id(0)
    for part, dpre in enumerate((dpre0, dpre1)):

        @pl.when(g // steps == part)
        def _():
            out[0] = lax.dot_general(
                dpre[...], w[...], (((1,), (1,)), ((), ())), preferred_element_type=F32
            ).astype(BF16)


def latent_gradient(dpre, w_hidden, tile=512):
    n, width = dpre[0].shape
    depth, points, steps = w_hidden.shape[0], 2 * n, n // tile
    return pl.pallas_call(
        functools.partial(latent_kernel, steps),
        grid=(2 * steps,),
        in_specs=[
            pl.BlockSpec((tile, width), lambda g: (jnp.minimum(g, steps - 1), 0)),
            pl.BlockSpec((tile, width), lambda g: (jnp.maximum(g - steps, 0), 0)),
            pl.BlockSpec((depth, width), lambda g: (0, 0)),
        ],
        out_specs=pl.BlockSpec((1, tile, depth), lambda g: (0, g, 0)),
        out_shape=jax.ShapeDtypeStruct((1, points, depth), BF16),
        compiler_params=params(),
        cost_estimate=cost(2 * points * width * depth, points * (2 * width + 2 * depth) + 2 * depth * width),
    )(*dpre, w_hidden)


def join_kernel(n_vars, where, *refs):
    ins, (grad_w, grad_o, grad_b, grad_b_out, loss, rest) = refs[:8], refs[8:]
    rows, half = ins[0].shape[0] - 32, ins[0].shape[1]
    for which in range(2):
        cols = pl.ds(pl.multiple_of(where[which] * half, half), half)
        for k in range(4):
            block = lax.rem(where[2 + which] - k + 4, 4)
            grad_w[pl.ds(pl.multiple_of(block * rows, rows), rows), cols] = ins[4 * which + k][0:rows, :]
            rest[pl.ds(pl.multiple_of(block * 32, 32), 32), cols] = ins[4 * which + k][rows : rows + 32, :]
    grad_o[...] = rest[0:n_vars, :]
    grad_b[...] = rest[n_vars : n_vars + 1, :]
    grad_b_out[...] = rest[n_vars + 1 : n_vars + 2, 0:n_vars]
    loss[...] = rest[n_vars + 2 : n_vars + 3, 0:1]


def join(where, own, sib, n_vars):
    rows, half = own[0].shape
    depth, width = 4 * (rows - 32), 2 * half
    vmem = pl.BlockSpec(memory_space=pltpu.VMEM)
    return pl.pallas_call(
        functools.partial(join_kernel, n_vars),
        in_specs=[pl.BlockSpec(memory_space=pltpu.SMEM)] + [vmem] * 8,
        out_specs=[vmem] * 5,
        out_shape=[
            jax.ShapeDtypeStruct((depth, width), F32),
            jax.ShapeDtypeStruct((n_vars, width), F32),
            jax.ShapeDtypeStruct((1, width), F32),
            jax.ShapeDtypeStruct((1, n_vars), F32),
            jax.ShapeDtypeStruct((1, 1), F32),
        ],
        scratch_shapes=[pltpu.VMEM((128, width), F32)],
        compiler_params=params(16),
        cost_estimate=cost(0, 8 * depth * width),
    )(where, *own, *sib)


def shards(latent, target, area_weight, var_weight, w_hidden, b_hidden, w_output, b_output):
    members = 4
    parts = [(0, 1024), (1, 1024)]
    n_vars, points = target.shape
    points_all = points * 32
    eps = 0.05 / members
    pair_coef = (1.0 - eps) / (members * (members - 1))
    scale = 1.0 / math.sqrt(members * points_all)
    loss_scale = 1.0 / (points_all * n_vars)
    core, x, z = lax.axis_index("core"), lax.axis_index("x"), lax.axis_index("z")
    place_own = jnp.where(core == 0, z, x)
    place_sib = jnp.where(core == 0, x, z)
    where = jnp.stack([core, 1 - core, place_own, place_sib]).astype(jnp.int32)
    own_latent = latent[0]
    made = [forward(part, n, own_latent, w_hidden, b_hidden, w_output, b_output) for part, n in parts]
    area, var = area_weight.reshape(1, points), var_weight.reshape(n_vars, 1)
    numbers = (members, scale, loss_scale, pair_coef)

    (pred0, hid0, sp0), (pred1, hid1, sp1) = made
    near0, near1 = send(pred0, NEAR), send(pred1, NEAR)
    sib0, sib1 = send(pred0, SWAP), send(pred1, SWAP)
    near0, sib0, sib1, where = lax.optimization_barrier((near0, sib0, sib1, where))
    others = (sib0, near0, send(near0, SWAP))
    dpre0, rest = cotangent(numbers, 0, pred0, others, target, area, var, sp0, hid0, w_output)
    near1, rest = lax.optimization_barrier((near1, rest))
    others = (sib1, near1, send(near1, SWAP))
    dpre1, rest, blocks_sib = cotangent_weight(
        numbers, 1, 1, where, pred1, others, target, area, var, sp1, hid1, w_output, rest, own_latent, dpre0
    )
    dpre = (dpre0, dpre1)
    blocks_own = weight_grad(0, where, own_latent, dpre, rest, scale)
    out_own, out_sib, latent_grad = grad_sum(blocks_own, blocks_sib, lambda d: latent_gradient(d, w_hidden), dpre)
    grad_w_hidden, grad_w_output, grad_b_hidden, grad_b_output, loss = join(where, out_own, out_sib, n_vars)
    return (
        loss.reshape(()),
        grad_w_hidden,
        grad_b_hidden.reshape(-1),
        grad_w_output,
        grad_b_output.reshape(-1),
        latent_grad,
    )


def solution(mesh):
    fine = Mesh(mesh.devices.reshape(2, 2, 2, 4, 4), ALL)
    member, space = ("ylo", "core"), ("yhi", "z", "x")
    return jax.shard_map(
        shards,
        mesh=fine,
        in_specs=(P(member, space, None), P(None, space), P(space), P(), P(), P(), P(), P()),
        out_specs=(P(), P(), P(), P(), P(), P(member, space, None)),
        check_vma=False,
    )
```

```python
import functools
import math

import jax
import jax.numpy as jnp
from jax import lax
from jax.experimental import pallas as pl
from jax.experimental.pallas import tpu as pltpu
from jax.sharding import Mesh, PartitionSpec as P

DELTA = 0.05
ALL = ("ylo", "core", "yhi", "z", "x")
MIB = 1 << 20
F32, BF16 = jnp.float32, jnp.bfloat16


def flat(core, x, y, z):
    return ((y % 2) * 2 + core) * 32 + (y // 2) * 16 + z * 4 + x


def moved(where):
    pairs = []
    for core in range(2):
        for x in range(4):
            for y in range(4):
                for z in range(4):
                    pairs.append((flat(core, x, y, z), flat(*where(core, x, y, z))))
    return pairs


SWAP = moved(lambda c, x, y, z: (1 - c, x, y, z))
NEAR = moved(lambda c, x, y, z: (c, x, y ^ 1, z))


def first(k):
    return moved(lambda c, x, y, z: (c, x, y, (z + k) % 4) if c == 0 else (c, (x + k) % 4, y, z))


def second(k):
    return moved(lambda c, x, y, z: (c, x, y, (z + k) % 4) if c == 1 else (c, (x + k) % 4, y, z))


def along_y(k):
    return moved(lambda c, x, y, z: (c, x, (y + k) % 4, z))


def send(array, pairs):
    return lax.ppermute(array, ALL, pairs)


def grad_sum(own, sibling, beside, dpre):
    core, x, z = lax.axis_index("core"), lax.axis_index("x"), lax.axis_index("z")
    place = jnp.where(core == 0, x, z)
    got = send(sibling, SWAP)
    held = {}
    for k in (2, 1, 3, 0):
        held[k], own, got = lax.optimization_barrier((own[k] + got[k], own, got))
    kept, dpre = lax.optimization_barrier((held[0], dpre))
    aside = beside(dpre)
    came = [send(held[k], first(k)) for k in (2, 1, 3)]
    came, aside = lax.optimization_barrier((came, aside))
    block = kept + came[0] + came[1] + came[2]
    rows = block.shape[0] // 4
    quarters = block.reshape((4, rows) + block.shape[1:])
    pick = lambda k: lax.dynamic_index_in_dim(quarters, (place + k) % 4, 0, keepdims=False)
    quarter = pick(0)
    for k in (1, 3, 2):
        quarter = quarter + send(pick(k), second(k))
    quarter = quarter + send(quarter, along_y(1)) + send(quarter, along_y(3)) + send(quarter, along_y(2))
    came = [quarter] + [send(quarter, second(k)) for k in (1, 2, 3)]
    twice = jnp.concatenate([came[3], came[2], came[1], came[0], came[3], came[2], came[1]], 0)
    block = lax.dynamic_slice_in_dim(twice, ((3 - place) % 4) * rows, 4 * rows, 0)
    mine = [block] + [send(block, first(k)) for k in (1, 2, 3)]
    return mine, [send(m, SWAP) for m in mine], aside


def params(mib=56):
    return pltpu.CompilerParams(vmem_limit_bytes=mib * MIB)


def cost(flops, moved_bytes, trans=0):
    return pl.CostEstimate(flops=flops, bytes_accessed=moved_bytes, transcendentals=trans)


def forward_kernel(lat, w, b_hid, w_out, b_out, pred, hid, slope_out):
    cols = 256
    for j in range(0, w.shape[1], cols):
        at = slice(j, j + cols)
        pre = jnp.dot(lat[...], w[:, at], preferred_element_type=F32) + b_hid[:, at]
        sig = jax.nn.sigmoid(pre)
        hid[:, at] = (pre * sig).astype(BF16)
        slope_out[:, at] = sig * (1.0 + pre * (1.0 - sig))
    n_vars = w_out.shape[0]
    bias = jnp.transpose(jnp.broadcast_to(b_out[...], (128, n_vars)))[:, 0:1]
    pred[...] = bias + lax.dot_general(w_out[...], hid[...], (((1,), (1,)), ((), ())), preferred_element_type=F32)


def forward(part, n, latent, w_hidden, b_hidden, w_output, b_output, tile=512):
    depth = latent.shape[1]
    width, n_vars = w_hidden.shape[1], w_output.shape[0]
    steps = n // tile
    whole = lambda shape: pl.BlockSpec(shape, lambda g: (0, 0))
    rows = pl.BlockSpec((tile, width), lambda g: (g, 0))
    return pl.pallas_call(
        forward_kernel,
        grid=(steps,),
        in_specs=[
            pl.BlockSpec((tile, depth), lambda g: (part * steps + g, 0)),
            whole(w_hidden.shape),
            whole((1, width)),
            whole(w_output.shape),
            whole((1, n_vars)),
        ],
        out_specs=[pl.BlockSpec((n_vars, tile), lambda g: (0, g)), rows, rows],
        out_shape=[
            jax.ShapeDtypeStruct((n_vars, n), F32),
            jax.ShapeDtypeStruct((n, width), BF16),
            jax.ShapeDtypeStruct((n, width), F32),
        ],
        compiler_params=params(),
        cost_estimate=cost(2 * n * width * (depth + n_vars), n * (2 * depth + 6 * width) + 2 * depth * width, 2 * n * width),
    )(latent, w_hidden, b_hidden.reshape(1, width), w_output, b_output.reshape(1, n_vars))


def cot_tile(members, scale, loss_scale, pair_coef, own, o1, o2, o3, target, area, var, sp, hid, w_out, rest):
    n_vars, n = own.shape
    weights = var[...] * area[...]
    mine = own[...]

    def both(diff):
        u = diff * diff + DELTA * DELTA
        r = lax.rsqrt(u)
        return u * r - DELTA, diff * r

    mag, slo = both(mine - target[...])
    pair_mag, pair_slo = jnp.zeros_like(mine), jnp.zeros_like(mine)
    for other in (o1, o2, o3):
        m, s = both(mine - other[...])
        pair_mag, pair_slo = pair_mag + m, pair_slo + s
    term = weights * (mag * (1.0 / members) - (0.5 * pair_coef) * pair_mag)
    cot = (weights * (slo * (1.0 / members) - pair_coef * pair_slo)).astype(BF16)
    sums = lax.dot_general(
        jnp.ones((16, n), BF16), cot, (((1,), (1,)), ((), ())), preferred_element_type=F32
    )[0:1]
    rest[n_vars + 1 : n_vars + 2, 0:n_vars] += sums * scale
    rest[n_vars + 2 : n_vars + 3, 0:128] += jnp.full((1, 128), jnp.sum(term) * loss_scale, F32)

    back = lax.dot_general(cot, w_out[...], (((0,), (0,)), ((), ())), preferred_element_type=F32)
    d = (back * sp[...]).astype(BF16)
    rest[0:n_vars, :] += jnp.dot(cot, hid[...], preferred_element_type=F32) * scale
    rest[n_vars : n_vars + 1, :] += jnp.sum(d.astype(F32), axis=0, keepdims=True) * scale
    return d


def cot_kernel(numbers, *refs):
    dpre, rest = refs[-2:]

    @pl.when(pl.program_id(0) == 0)
    def _():
        rest[...] = jnp.zeros_like(rest)

    dpre[...] = cot_tile(*numbers, *refs[:10], rest)


def block_copies(which, where, lat, held, sems, dpre, to):
    rows, half = held.shape[2], to.shape[1]
    cols = pl.ds(pl.multiple_of(where[which] * half, half), half)

    def columns(k):
        block = lax.rem(where[2 + which] + k, 4)
        at = pl.ds(pl.multiple_of(block * rows, rows), rows)
        return pltpu.make_async_copy(lat.at[:, at], held.at[k], sems.at[k])

    return columns, pltpu.make_async_copy(dpre.at[:, cols], to, sems.at[4])


def weight_block(scale, which, where, k, lat, dpres, rest, out, j=0):
    rows, half = lat.shape[1], out.shape[2]
    total, start = 0.0, 0
    for d in dpres:
        n = d.shape[0]
        total += lax.dot_general(lat[start : start + n, :], d, (((0,), (0,)), ((), ())), preferred_element_type=F32)
        start += n
    block = lax.rem(where[2 + which] + k, 4)
    out[j, 0:rows, :] = total * scale
    cols = pl.ds(pl.multiple_of(where[which] * half, half), half)
    out[j, rows : rows + 32, :] = rest[pl.ds(pl.multiple_of(block * 32, 32), 32), cols]


def cot_weight_kernel(numbers, steps, which, where, *refs):
    ins, (rest_in, lat, dpre0), (dpre, rest, out, mine, lat_held, half0, sems) = refs[:10], refs[10:13], refs[13:]
    g = pl.program_id(0)
    tile, half = dpre.shape[0], out.shape[2]
    columns, first_half = block_copies(which, where, lat, lat_held, sems, dpre0, half0)

    @pl.when(g == 0)
    def _():
        first_half.start()
        for k in range(4):
            columns(k).start()
        rest[...] = rest_in[...]

    @pl.when(g < steps)
    def _():
        d = cot_tile(*numbers, *ins, rest)
        dpre[...] = d
        mine[pl.ds(pl.multiple_of(g * tile, tile), tile), :] = d

    @pl.when(g == steps)
    def _():
        first_half.wait()

    @pl.when(g >= steps)
    def _():
        for j in range(out.shape[0]):
            columns(out.shape[0] * (g - steps) + j).wait()
        cols = pl.ds(pl.multiple_of(where[which] * half, half), half)
        dpres = (half0[...], mine[:, cols])
        for j in range(out.shape[0]):
            k = out.shape[0] * (g - steps) + j
            weight_block(numbers[1], which, where, k, lat_held.at[k], dpres, rest, out, j)


def cotangent(numbers, part, own, others, target, area, var, sp, hid, w_output, tile=512):
    n, width = sp.shape
    n_vars, steps = target.shape[0], n // tile
    whole = lambda shape: pl.BlockSpec(shape, lambda g: (0, 0))
    local = pl.BlockSpec((n_vars, tile), lambda g: (0, g))
    rows = pl.BlockSpec((tile, width), lambda g: (g, 0))
    return pl.pallas_call(
        functools.partial(cot_kernel, numbers),
        grid=(steps,),
        in_specs=[local] * 4
        + [
            pl.BlockSpec((n_vars, tile), lambda g: (0, part * steps + g)),
            pl.BlockSpec((1, tile), lambda g: (0, part * steps + g)),
            whole((n_vars, 1)),
            rows,
            rows,
            whole(w_output.shape),
        ],
        out_specs=[rows, whole((128, width))],
        out_shape=[
            jax.ShapeDtypeStruct((n, width), BF16),
            jax.ShapeDtypeStruct((128, width), F32),
        ],
        compiler_params=params(),
        cost_estimate=cost(1, 1),
    )(own, *others, target, area, var, sp, hid, w_output)


def cotangent_weight(
    numbers, part, which, where, own, others, target, area, var, sp, hid, w_output, rest, latent, dpre0, tile=512
):
    n, width = sp.shape
    points, depth = latent.shape
    n_vars, steps, half, block = target.shape[0], n // tile, width // 2, depth // 4
    at = lambda g: jnp.minimum(g, steps - 1)
    step = lambda g: jnp.maximum(g - steps, 0)
    whole = lambda shape: pl.BlockSpec(shape, lambda g, s: (0, 0))
    local = pl.BlockSpec((n_vars, tile), lambda g, s: (0, at(g)))
    rows = pl.BlockSpec((tile, width), lambda g, s: (at(g), 0))
    hbm = pl.BlockSpec(memory_space=pl.ANY)
    return pl.pallas_call(
        functools.partial(cot_weight_kernel, numbers, steps, which),
        grid_spec=pltpu.PrefetchScalarGridSpec(
            num_scalar_prefetch=1,
            grid=(steps + 2,),
            in_specs=[local] * 4
            + [
                pl.BlockSpec((n_vars, tile), lambda g, s: (0, part * steps + at(g))),
                pl.BlockSpec((1, tile), lambda g, s: (0, part * steps + at(g))),
                whole((n_vars, 1)),
                rows,
                rows,
                whole(w_output.shape),
                whole((128, width)),
                hbm,
                hbm,
            ],
            out_specs=[rows, whole((128, width)), pl.BlockSpec((2, block + 32, half), lambda g, s: (step(g), 0, 0))],
            scratch_shapes=[
                pltpu.VMEM((n, width), BF16),
                pltpu.VMEM((4, points, block), BF16),
                pltpu.VMEM((points - n, half), BF16),
                pltpu.SemaphoreType.DMA((5,)),
            ],
        ),
        out_shape=[
            jax.ShapeDtypeStruct((n, width), BF16),
            jax.ShapeDtypeStruct((128, width), F32),
            jax.ShapeDtypeStruct((4, block + 32, half), F32),
        ],
        compiler_params=params(),
        cost_estimate=cost(2 * points * half * depth, points * 2 * depth + n * (n_vars * 20 + 8 * width) + 4 * depth * half),
    )(where, own, *others, target, area, var, sp, hid, w_output, rest, latent, dpre0)


def weight_kernel(scale, which, where, lat0, lat1, dpre0, dpre1, rest, out):
    for j, lat in enumerate((lat0, lat1)):
        weight_block(scale, which, where, 2 * pl.program_id(0) + j, lat, (dpre0[...], dpre1[...]), rest, out, j)


def weight_grad(which, where, latent, dpre, rest, scale):
    (points, depth), width = latent.shape, dpre[0].shape[1]
    half, rows = width // 2, depth // 4
    halves = pl.BlockSpec((points // 2, half), lambda g, s: (0, s[which]))
    lat = lambda j: pl.BlockSpec((points, rows), lambda g, s: (0, lax.rem(s[2 + which] + 2 * g + j, 4)))
    return pl.pallas_call(
        functools.partial(weight_kernel, scale, which),
        grid_spec=pltpu.PrefetchScalarGridSpec(
            num_scalar_prefetch=1,
            grid=(2,),
            in_specs=[
                lat(0),
                lat(1),
                halves,
                halves,
                pl.BlockSpec((128, width), lambda g, s: (0, 0)),
            ],
            out_specs=pl.BlockSpec((2, rows + 32, half), lambda g, s: (g, 0, 0)),
        ),
        out_shape=jax.ShapeDtypeStruct((4, rows + 32, half), F32),
        compiler_params=params(),
        cost_estimate=cost(2 * points * half * depth, points * (2 * half + 2 * depth) + 4 * depth * half),
    )(where, latent, latent, *dpre, rest)


def latent_kernel(steps, dpre0, dpre1, w, out):
    g = pl.program_id(0)
    for part, dpre in enumerate((dpre0, dpre1)):

        @pl.when(g // steps == part)
        def _():
            out[0] = lax.dot_general(
                dpre[...], w[...], (((1,), (1,)), ((), ())), preferred_element_type=F32
            ).astype(BF16)


def latent_gradient(dpre, w_hidden, tile=512):
    n, width = dpre[0].shape
    depth, points, steps = w_hidden.shape[0], 2 * n, n // tile
    return pl.pallas_call(
        functools.partial(latent_kernel, steps),
        grid=(2 * steps,),
        in_specs=[
            pl.BlockSpec((tile, width), lambda g: (jnp.minimum(g, steps - 1), 0)),
            pl.BlockSpec((tile, width), lambda g: (jnp.maximum(g - steps, 0), 0)),
            pl.BlockSpec((depth, width), lambda g: (0, 0)),
        ],
        out_specs=pl.BlockSpec((1, tile, depth), lambda g: (0, g, 0)),
        out_shape=jax.ShapeDtypeStruct((1, points, depth), BF16),
        compiler_params=params(),
        cost_estimate=cost(2 * points * width * depth, points * (2 * width + 2 * depth) + 2 * depth * width),
    )(*dpre, w_hidden)


def join_kernel(n_vars, where, *refs):
    ins, (grad_w, grad_o, grad_b, grad_b_out, loss, rest) = refs[:8], refs[8:]
    rows, half = ins[0].shape[0] - 32, ins[0].shape[1]
    for which in range(2):
        cols = pl.ds(pl.multiple_of(where[which] * half, half), half)
        for k in range(4):
            block = lax.rem(where[2 + which] - k + 4, 4)
            grad_w[pl.ds(pl.multiple_of(block * rows, rows), rows), cols] = ins[4 * which + k][0:rows, :]
            rest[pl.ds(pl.multiple_of(block * 32, 32), 32), cols] = ins[4 * which + k][rows : rows + 32, :]
    grad_o[...] = rest[0:n_vars, :]
    grad_b[...] = rest[n_vars : n_vars + 1, :]
    grad_b_out[...] = rest[n_vars + 1 : n_vars + 2, 0:n_vars]
    loss[...] = rest[n_vars + 2 : n_vars + 3, 0:1]


def join(where, own, sib, n_vars):
    rows, half = own[0].shape
    depth, width = 4 * (rows - 32), 2 * half
    vmem = pl.BlockSpec(memory_space=pltpu.VMEM)
    return pl.pallas_call(
        functools.partial(join_kernel, n_vars),
        in_specs=[pl.BlockSpec(memory_space=pltpu.SMEM)] + [vmem] * 8,
        out_specs=[vmem] * 5,
        out_shape=[
            jax.ShapeDtypeStruct((depth, width), F32),
            jax.ShapeDtypeStruct((n_vars, width), F32),
            jax.ShapeDtypeStruct((1, width), F32),
            jax.ShapeDtypeStruct((1, n_vars), F32),
            jax.ShapeDtypeStruct((1, 1), F32),
        ],
        scratch_shapes=[pltpu.VMEM((128, width), F32)],
        compiler_params=params(16),
        cost_estimate=cost(0, 8 * depth * width),
    )(where, *own, *sib)


def shards(latent, target, area_weight, var_weight, w_hidden, b_hidden, w_output, b_output):
    members = 4
    parts = [(0, 1024), (1, 1024)]
    n_vars, points = target.shape
    points_all = points * 32
    eps = 0.05 / members
    pair_coef = (1.0 - eps) / (members * (members - 1))
    scale = 1.0 / math.sqrt(members * points_all)
    loss_scale = 1.0 / (points_all * n_vars)
    core, x, z = lax.axis_index("core"), lax.axis_index("x"), lax.axis_index("z")
    place_own = jnp.where(core == 0, z, x)
    place_sib = jnp.where(core == 0, x, z)
    where = jnp.stack([core, 1 - core, place_own, place_sib]).astype(jnp.int32)
    own_latent = latent[0]
    made = [forward(part, n, own_latent, w_hidden, b_hidden, w_output, b_output) for part, n in parts]
    area, var = area_weight.reshape(1, points), var_weight.reshape(n_vars, 1)
    numbers = (members, scale, loss_scale, pair_coef)

    (pred0, hid0, sp0), (pred1, hid1, sp1) = made
    near0, near1 = send(pred0, NEAR), send(pred1, NEAR)
    sib0, sib1 = send(pred0, SWAP), send(pred1, SWAP)
    near0, sib0, sib1, where = lax.optimization_barrier((near0, sib0, sib1, where))
    others = (sib0, near0, send(near0, SWAP))
    dpre0, rest = cotangent(numbers, 0, pred0, others, target, area, var, sp0, hid0, w_output)
    near1, rest = lax.optimization_barrier((near1, rest))
    others = (sib1, near1, send(near1, SWAP))
    dpre1, rest, blocks_sib = cotangent_weight(
        numbers, 1, 1, where, pred1, others, target, area, var, sp1, hid1, w_output, rest, own_latent, dpre0
    )
    dpre = (dpre0, dpre1)
    blocks_own = weight_grad(0, where, own_latent, dpre, rest, scale)
    out_own, out_sib, latent_grad = grad_sum(blocks_own, blocks_sib, lambda d: latent_gradient(d, w_hidden), dpre)
    grad_w_hidden, grad_w_output, grad_b_hidden, grad_b_output, loss = join(where, out_own, out_sib, n_vars)
    return (
        loss.reshape(()),
        grad_w_hidden,
        grad_b_hidden.reshape(-1),
        grad_w_output,
        grad_b_output.reshape(-1),
        latent_grad,
    )


def solution(mesh):
    fine = Mesh(mesh.devices.reshape(2, 2, 2, 4, 4), ALL)
    member, space = ("ylo", "core"), ("yhi", "z", "x")
    return jax.shard_map(
        shards,
        mesh=fine,
        in_specs=(P(member, space, None), P(None, space), P(space), P(), P(), P(), P(), P()),
        out_specs=(P(), P(), P(), P(), P(), P(member, space, None)),
        check_vma=False,
    )
```

```python
import functools
import math

import jax
import jax.numpy as jnp
from jax import lax
from jax.experimental import pallas as pl
from jax.experimental.pallas import tpu as pltpu
from jax.sharding import Mesh, PartitionSpec as P

DELTA = 0.05
ALL = ("ylo", "core", "yhi", "z", "x")
MIB = 1 << 20
F32, BF16 = jnp.float32, jnp.bfloat16


def flat(core, x, y, z):
    return ((y % 2) * 2 + core) * 32 + (y // 2) * 16 + z * 4 + x


def moved(where):
    pairs = []
    for core in range(2):
        for x in range(4):
            for y in range(4):
                for z in range(4):
                    pairs.append((flat(core, x, y, z), flat(*where(core, x, y, z))))
    return pairs


SWAP = moved(lambda c, x, y, z: (1 - c, x, y, z))
NEAR = moved(lambda c, x, y, z: (c, x, y ^ 1, z))


def first(k):
    return moved(lambda c, x, y, z: (c, x, y, (z + k) % 4) if c == 0 else (c, (x + k) % 4, y, z))


def second(k):
    return moved(lambda c, x, y, z: (c, x, y, (z + k) % 4) if c == 1 else (c, (x + k) % 4, y, z))


def along_y(k):
    return moved(lambda c, x, y, z: (c, x, (y + k) % 4, z))


def send(array, pairs):
    return lax.ppermute(array, ALL, pairs)


def grad_sum(own, sibling, beside, dpre):
    core, x, z = lax.axis_index("core"), lax.axis_index("x"), lax.axis_index("z")
    place = jnp.where(core == 0, x, z)
    got = send(sibling, SWAP)
    held = {}
    for k in (2, 1, 3, 0):
        held[k], own, got = lax.optimization_barrier((own[k] + got[k], own, got))
    kept, dpre = lax.optimization_barrier((held[0], dpre))
    aside = beside(dpre)
    came = [send(held[k], first(k)) for k in (2, 1, 3)]
    came, aside = lax.optimization_barrier((came, aside))
    block = kept + came[0] + came[1] + came[2]
    rows = block.shape[0] // 4
    quarters = block.reshape((4, rows) + block.shape[1:])
    pick = lambda k: lax.dynamic_index_in_dim(quarters, (place + k) % 4, 0, keepdims=False)
    quarter = pick(0)
    for k in (1, 3, 2):
        quarter = quarter + send(pick(k), second(k))
    quarter = quarter + send(quarter, along_y(1)) + send(quarter, along_y(3)) + send(quarter, along_y(2))
    came = [quarter] + [send(quarter, second(k)) for k in (1, 2, 3)]
    twice = jnp.concatenate([came[3], came[2], came[1], came[0], came[3], came[2], came[1]], 0)
    block = lax.dynamic_slice_in_dim(twice, ((3 - place) % 4) * rows, 4 * rows, 0)
    mine = [block] + [send(block, first(k)) for k in (1, 2, 3)]
    return mine, [send(m, SWAP) for m in mine], aside


def params(mib=56):
    return pltpu.CompilerParams(vmem_limit_bytes=mib * MIB)


def cost(flops, moved_bytes, trans=0):
    return pl.CostEstimate(flops=flops, bytes_accessed=moved_bytes, transcendentals=trans)


def forward_kernel(lat, w, b_hid, w_out, b_out, pred, hid, slope_out):
    cols = 256
    for j in range(0, w.shape[1], cols):
        at = slice(j, j + cols)
        pre = jnp.dot(lat[...], w[:, at], preferred_element_type=F32) + b_hid[:, at]
        sig = jax.nn.sigmoid(pre)
        hid[:, at] = (pre * sig).astype(BF16)
        slope_out[:, at] = sig * (1.0 + pre * (1.0 - sig))
    n_vars = w_out.shape[0]
    bias = jnp.transpose(jnp.broadcast_to(b_out[...], (128, n_vars)))[:, 0:1]
    pred[...] = bias + lax.dot_general(w_out[...], hid[...], (((1,), (1,)), ((), ())), preferred_element_type=F32)


def forward(part, n, latent, w_hidden, b_hidden, w_output, b_output, tile=512):
    depth = latent.shape[1]
    width, n_vars = w_hidden.shape[1], w_output.shape[0]
    steps = n // tile
    whole = lambda shape: pl.BlockSpec(shape, lambda g: (0, 0))
    rows = pl.BlockSpec((tile, width), lambda g: (g, 0))
    return pl.pallas_call(
        forward_kernel,
        grid=(steps,),
        in_specs=[
            pl.BlockSpec((tile, depth), lambda g: (part * steps + g, 0)),
            whole(w_hidden.shape),
            whole((1, width)),
            whole(w_output.shape),
            whole((1, n_vars)),
        ],
        out_specs=[pl.BlockSpec((n_vars, tile), lambda g: (0, g)), rows, rows],
        out_shape=[
            jax.ShapeDtypeStruct((n_vars, n), F32),
            jax.ShapeDtypeStruct((n, width), BF16),
            jax.ShapeDtypeStruct((n, width), F32),
        ],
        compiler_params=params(),
        cost_estimate=cost(2 * n * width * (depth + n_vars), n * (2 * depth + 6 * width) + 2 * depth * width, 2 * n * width),
    )(latent, w_hidden, b_hidden.reshape(1, width), w_output, b_output.reshape(1, n_vars))


def cot_tile(members, scale, loss_scale, pair_coef, own, o1, o2, o3, target, area, var, sp, hid, w_out, rest):
    n_vars, n = own.shape
    weights = var[...] * area[...]
    mine = own[...]

    def both(diff):
        u = diff * diff + DELTA * DELTA
        r = lax.rsqrt(u)
        return u * r - DELTA, diff * r

    mag, slo = both(mine - target[...])
    pair_mag, pair_slo = jnp.zeros_like(mine), jnp.zeros_like(mine)
    for other in (o1, o2, o3):
        m, s = both(mine - other[...])
        pair_mag, pair_slo = pair_mag + m, pair_slo + s
    term = weights * (mag * (1.0 / members) - (0.5 * pair_coef) * pair_mag)
    cot = (weights * (slo * (1.0 / members) - pair_coef * pair_slo)).astype(BF16)
    sums = lax.dot_general(
        jnp.ones((16, n), BF16), cot, (((1,), (1,)), ((), ())), preferred_element_type=F32
    )[0:1]
    rest[n_vars + 1 : n_vars + 2, 0:n_vars] += sums * scale
    rest[n_vars + 2 : n_vars + 3, 0:128] += jnp.full((1, 128), jnp.sum(term) * loss_scale, F32)

    back = lax.dot_general(cot, w_out[...], (((0,), (0,)), ((), ())), preferred_element_type=F32)
    d = (back * sp[...]).astype(BF16)
    rest[0:n_vars, :] += jnp.dot(cot, hid[...], preferred_element_type=F32) * scale
    rest[n_vars : n_vars + 1, :] += jnp.sum(d.astype(F32), axis=0, keepdims=True) * scale
    return d


def cot_kernel(numbers, *refs):
    dpre, rest = refs[-2:]

    @pl.when(pl.program_id(0) == 0)
    def _():
        rest[...] = jnp.zeros_like(rest)

    dpre[...] = cot_tile(*numbers, *refs[:10], rest)


def block_copies(which, where, lat, held, sems, dpre, to):
    rows, half = held.shape[2], to.shape[1]
    cols = pl.ds(pl.multiple_of(where[which] * half, half), half)

    def columns(k):
        block = lax.rem(where[2 + which] + k, 4)
        at = pl.ds(pl.multiple_of(block * rows, rows), rows)
        return pltpu.make_async_copy(lat.at[:, at], held.at[k], sems.at[k])

    return columns, pltpu.make_async_copy(dpre.at[:, cols], to, sems.at[4])


def weight_block(scale, which, where, k, lat, dpres, rest, out, j=0):
    rows, half = lat.shape[1], out.shape[2]
    total, start = 0.0, 0
    for d in dpres:
        n = d.shape[0]
        total += lax.dot_general(lat[start : start + n, :], d, (((0,), (0,)), ((), ())), preferred_element_type=F32)
        start += n
    block = lax.rem(where[2 + which] + k, 4)
    out[j, 0:rows, :] = total * scale
    cols = pl.ds(pl.multiple_of(where[which] * half, half), half)
    out[j, rows : rows + 32, :] = rest[pl.ds(pl.multiple_of(block * 32, 32), 32), cols]


def cot_weight_kernel(numbers, steps, which, where, *refs):
    ins, (rest_in, lat, dpre0), (dpre, rest, out, mine, lat_held, half0, sems) = refs[:10], refs[10:13], refs[13:]
    g = pl.program_id(0)
    tile, half = dpre.shape[0], out.shape[2]
    columns, first_half = block_copies(which, where, lat, lat_held, sems, dpre0, half0)

    @pl.when(g == 0)
    def _():
        first_half.start()
        for k in range(4):
            columns(k).start()
        rest[...] = rest_in[...]

    @pl.when(g < steps)
    def _():
        d = cot_tile(*numbers, *ins, rest)
        dpre[...] = d
        mine[pl.ds(pl.multiple_of(g * tile, tile), tile), :] = d

    @pl.when(g == steps)
    def _():
        first_half.wait()

    @pl.when(g >= steps)
    def _():
        for j in range(out.shape[0]):
            columns(out.shape[0] * (g - steps) + j).wait()
        cols = pl.ds(pl.multiple_of(where[which] * half, half), half)
        dpres = (half0[...], mine[:, cols])
        for j in range(out.shape[0]):
            k = out.shape[0] * (g - steps) + j
            weight_block(numbers[1], which, where, k, lat_held.at[k], dpres, rest, out, j)


def cotangent(numbers, part, own, others, target, area, var, sp, hid, w_output, tile=512):
    n, width = sp.shape
    n_vars, steps = target.shape[0], n // tile
    whole = lambda shape: pl.BlockSpec(shape, lambda g: (0, 0))
    local = pl.BlockSpec((n_vars, tile), lambda g: (0, g))
    rows = pl.BlockSpec((tile, width), lambda g: (g, 0))
    return pl.pallas_call(
        functools.partial(cot_kernel, numbers),
        grid=(steps,),
        in_specs=[local] * 4
        + [
            pl.BlockSpec((n_vars, tile), lambda g: (0, part * steps + g)),
            pl.BlockSpec((1, tile), lambda g: (0, part * steps + g)),
            whole((n_vars, 1)),
            rows,
            rows,
            whole(w_output.shape),
        ],
        out_specs=[rows, whole((128, width))],
        out_shape=[
            jax.ShapeDtypeStruct((n, width), BF16),
            jax.ShapeDtypeStruct((128, width), F32),
        ],
        compiler_params=params(),
        cost_estimate=cost(1, 1),
    )(own, *others, target, area, var, sp, hid, w_output)


def cotangent_weight(
    numbers, part, which, where, own, others, target, area, var, sp, hid, w_output, rest, latent, dpre0, tile=512
):
    n, width = sp.shape
    points, depth = latent.shape
    n_vars, steps, half, block = target.shape[0], n // tile, width // 2, depth // 4
    at = lambda g: jnp.minimum(g, steps - 1)
    step = lambda g: jnp.maximum(g - steps, 0)
    whole = lambda shape: pl.BlockSpec(shape, lambda g, s: (0, 0))
    local = pl.BlockSpec((n_vars, tile), lambda g, s: (0, at(g)))
    rows = pl.BlockSpec((tile, width), lambda g, s: (at(g), 0))
    hbm = pl.BlockSpec(memory_space=pl.ANY)
    return pl.pallas_call(
        functools.partial(cot_weight_kernel, numbers, steps, which),
        grid_spec=pltpu.PrefetchScalarGridSpec(
            num_scalar_prefetch=1,
            grid=(steps + 2,),
            in_specs=[local] * 4
            + [
                pl.BlockSpec((n_vars, tile), lambda g, s: (0, part * steps + at(g))),
                pl.BlockSpec((1, tile), lambda g, s: (0, part * steps + at(g))),
                whole((n_vars, 1)),
                rows,
                rows,
                whole(w_output.shape),
                whole((128, width)),
                hbm,
                hbm,
            ],
            out_specs=[rows, whole((128, width)), pl.BlockSpec((2, block + 32, half), lambda g, s: (step(g), 0, 0))],
            scratch_shapes=[
                pltpu.VMEM((n, width), BF16),
                pltpu.VMEM((4, points, block), BF16),
                pltpu.VMEM((points - n, half), BF16),
                pltpu.SemaphoreType.DMA((5,)),
            ],
        ),
        out_shape=[
            jax.ShapeDtypeStruct((n, width), BF16),
            jax.ShapeDtypeStruct((128, width), F32),
            jax.ShapeDtypeStruct((4, block + 32, half), F32),
        ],
        compiler_params=params(52),
        cost_estimate=cost(2 * points * half * depth, points * 2 * depth + n * (n_vars * 20 + 8 * width) + 4 * depth * half),
    )(where, own, *others, target, area, var, sp, hid, w_output, rest, latent, dpre0)


def weight_kernel(scale, which, where, lat0, lat1, dpre0, dpre1, rest, out):
    for j, lat in enumerate((lat0, lat1)):
        weight_block(scale, which, where, 2 * pl.program_id(0) + j, lat, (dpre0[...], dpre1[...]), rest, out, j)


def weight_grad(which, where, latent, dpre, rest, scale):
    (points, depth), width = latent.shape, dpre[0].shape[1]
    half, rows = width // 2, depth // 4
    halves = pl.BlockSpec((points // 2, half), lambda g, s: (0, s[which]))
    lat = lambda j: pl.BlockSpec((points, rows), lambda g, s: (0, lax.rem(s[2 + which] + 2 * g + j, 4)))
    return pl.pallas_call(
        functools.partial(weight_kernel, scale, which),
        grid_spec=pltpu.PrefetchScalarGridSpec(
            num_scalar_prefetch=1,
            grid=(2,),
            in_specs=[
                lat(0),
                lat(1),
                halves,
                halves,
                pl.BlockSpec((128, width), lambda g, s: (0, 0)),
            ],
            out_specs=pl.BlockSpec((2, rows + 32, half), lambda g, s: (g, 0, 0)),
        ),
        out_shape=jax.ShapeDtypeStruct((4, rows + 32, half), F32),
        compiler_params=params(),
        cost_estimate=cost(2 * points * half * depth, points * (2 * half + 2 * depth) + 4 * depth * half),
    )(where, latent, latent, *dpre, rest)


def latent_kernel(steps, dpre0, dpre1, w, out):
    g = pl.program_id(0)
    for part, dpre in enumerate((dpre0, dpre1)):

        @pl.when(g // steps == part)
        def _():
            out[0] = lax.dot_general(
                dpre[...], w[...], (((1,), (1,)), ((), ())), preferred_element_type=F32
            ).astype(BF16)


def latent_gradient(dpre, w_hidden, tile=512):
    n, width = dpre[0].shape
    depth, points, steps = w_hidden.shape[0], 2 * n, n // tile
    return pl.pallas_call(
        functools.partial(latent_kernel, steps),
        grid=(2 * steps,),
        in_specs=[
            pl.BlockSpec((tile, width), lambda g: (jnp.minimum(g, steps - 1), 0)),
            pl.BlockSpec((tile, width), lambda g: (jnp.maximum(g - steps, 0), 0)),
            pl.BlockSpec((depth, width), lambda g: (0, 0)),
        ],
        out_specs=pl.BlockSpec((1, tile, depth), lambda g: (0, g, 0)),
        out_shape=jax.ShapeDtypeStruct((1, points, depth), BF16),
        compiler_params=params(),
        cost_estimate=cost(2 * points * width * depth, points * (2 * width + 2 * depth) + 2 * depth * width),
    )(*dpre, w_hidden)


def join_kernel(n_vars, where, *refs):
    ins, (grad_w, grad_o, grad_b, grad_b_out, loss, rest) = refs[:8], refs[8:]
    rows, half = ins[0].shape[0] - 32, ins[0].shape[1]
    for which in range(2):
        cols = pl.ds(pl.multiple_of(where[which] * half, half), half)
        for k in range(4):
            block = lax.rem(where[2 + which] - k + 4, 4)
            grad_w[pl.ds(pl.multiple_of(block * rows, rows), rows), cols] = ins[4 * which + k][0:rows, :]
            rest[pl.ds(pl.multiple_of(block * 32, 32), 32), cols] = ins[4 * which + k][rows : rows + 32, :]
    grad_o[...] = rest[0:n_vars, :]
    grad_b[...] = rest[n_vars : n_vars + 1, :]
    grad_b_out[...] = rest[n_vars + 1 : n_vars + 2, 0:n_vars]
    loss[...] = rest[n_vars + 2 : n_vars + 3, 0:1]


def join(where, own, sib, n_vars):
    rows, half = own[0].shape
    depth, width = 4 * (rows - 32), 2 * half
    vmem = pl.BlockSpec(memory_space=pltpu.VMEM)
    return pl.pallas_call(
        functools.partial(join_kernel, n_vars),
        in_specs=[pl.BlockSpec(memory_space=pltpu.SMEM)] + [vmem] * 8,
        out_specs=[vmem] * 5,
        out_shape=[
            jax.ShapeDtypeStruct((depth, width), F32),
            jax.ShapeDtypeStruct((n_vars, width), F32),
            jax.ShapeDtypeStruct((1, width), F32),
            jax.ShapeDtypeStruct((1, n_vars), F32),
            jax.ShapeDtypeStruct((1, 1), F32),
        ],
        scratch_shapes=[pltpu.VMEM((128, width), F32)],
        compiler_params=params(16),
        cost_estimate=cost(0, 8 * depth * width),
    )(where, *own, *sib)


def shards(latent, target, area_weight, var_weight, w_hidden, b_hidden, w_output, b_output):
    members = 4
    parts = [(0, 1024), (1, 1024)]
    n_vars, points = target.shape
    points_all = points * 32
    eps = 0.05 / members
    pair_coef = (1.0 - eps) / (members * (members - 1))
    scale = 1.0 / math.sqrt(members * points_all)
    loss_scale = 1.0 / (points_all * n_vars)
    core, x, z = lax.axis_index("core"), lax.axis_index("x"), lax.axis_index("z")
    place_own = jnp.where(core == 0, z, x)
    place_sib = jnp.where(core == 0, x, z)
    where = jnp.stack([core, 1 - core, place_own, place_sib]).astype(jnp.int32)
    own_latent = latent[0]
    made = [forward(part, n, own_latent, w_hidden, b_hidden, w_output, b_output) for part, n in parts]
    area, var = area_weight.reshape(1, points), var_weight.reshape(n_vars, 1)
    numbers = (members, scale, loss_scale, pair_coef)

    (pred0, hid0, sp0), (pred1, hid1, sp1) = made
    near0, near1 = send(pred0, NEAR), send(pred1, NEAR)
    sib0, sib1 = send(pred0, SWAP), send(pred1, SWAP)
    near0, sib0, sib1, where = lax.optimization_barrier((near0, sib0, sib1, where))
    others = (sib0, near0, send(near0, SWAP))
    dpre0, rest = cotangent(numbers, 0, pred0, others, target, area, var, sp0, hid0, w_output)
    near1, rest = lax.optimization_barrier((near1, rest))
    others = (sib1, near1, send(near1, SWAP))
    dpre1, rest, blocks_sib = cotangent_weight(
        numbers, 1, 1, where, pred1, others, target, area, var, sp1, hid1, w_output, rest, own_latent, dpre0
    )
    dpre = (dpre0, dpre1)
    blocks_own = weight_grad(0, where, own_latent, dpre, rest, scale)
    out_own, out_sib, latent_grad = grad_sum(blocks_own, blocks_sib, lambda d: latent_gradient(d, w_hidden), dpre)
    grad_w_hidden, grad_w_output, grad_b_hidden, grad_b_output, loss = join(where, out_own, out_sib, n_vars)
    return (
        loss.reshape(()),
        grad_w_hidden,
        grad_b_hidden.reshape(-1),
        grad_w_output,
        grad_b_output.reshape(-1),
        latent_grad,
    )


def solution(mesh):
    fine = Mesh(mesh.devices.reshape(2, 2, 2, 4, 4), ALL)
    member, space = ("ylo", "core"), ("yhi", "z", "x")
    return jax.shard_map(
        shards,
        mesh=fine,
        in_specs=(P(member, space, None), P(None, space), P(space), P(), P(), P(), P(), P()),
        out_specs=(P(), P(), P(), P(), P(), P(member, space, None)),
        check_vma=False,
    )
```
